256 devices in a mesh: space: 64 (over x, y_hi, z), kern: 4 (over y_lo, core).
Axes of the slice: x: 4, y: 4 (y_hi: 2, y_lo: 2; y = y_hi * 2 + y_lo), z: 8, core: 2. Of those that a mesh axis runs over, the one named last changes fastest.
Arguments:
- phase: float32 [512, 8192], P(None, 'space'), may hold values from -3.140625 to 3.140625
- target: int32 [512, 8192], P(None, 'space'), may hold values 0 or 1
- kernels: float32 [2, 16, 129, 129], P(None, 'kern'), may hold values from -0.046875 to 0.046875
- weights: float32 [16], P('kern'), may hold values from 0.01 to 0.25
Outputs:
- resist: float32 [512, 8192], P('kern', 'space')
- grad_phase: float32 [512, 8192], P('kern', 'space')
The draws below stay inside these ranges and needn't reach their ends.
All inputs are finite; a program needn't handle non-finite values. No bound on the sum of `target` on one device may be relied on, other than what follows from the above.
Results may differ from the reference program's by a relative error of at most 0.0003.
Values sent between devices are 32-bit elements; how exact they have to be, the bound alone decides.
A program may use at most 64 MiB of HBM per device.

```python
import math
import jax
import jax.numpy as jnp
from jax import lax

ROWS = 512
SUPPORT = 129
KERNELS = 16
HALF = 64
COLUMNS = 8192


def with_ends(array, own_key, low, high):
    longest = array.shape.index(max(array.shape))
    spots = []
    for shift in (0, 1):
        where = [jax.random.randint(jax.random.fold_in(own_key, axis), (), 0, length) for axis, length in enumerate(array.shape)]
        where[longest] = (where[longest] + shift) % array.shape[longest]
        spots.append(tuple(where))
    return array.at[spots[0]].set(low).at[spots[1]].set(high)


def block_levels(stream_key, extent, pieces, smallest, high):
    loudness, own = 1.0, jax.random.fold_in(stream_key, 6)
    for axis_at, blocks in pieces:
        draws = jnp.exp(jax.random.uniform(jax.random.fold_in(own, axis_at), (blocks,), jnp.float32, smallest / len(pieces), high / len(pieces)))
        loudness = loudness * jnp.repeat(draws, extent[axis_at] // blocks).reshape([-1 if axis == axis_at else 1 for axis in range(len(extent))])
    return loudness


def centred(key, shape, width, limit, cuts=(), kind=jnp.bfloat16):
    gain = block_levels(key, shape, cuts, -0.22, 0.18) if cuts else 1.0
    drawn = jax.random.normal(key, shape, jnp.float32) * width * gain
    return jnp.minimum(jnp.maximum(drawn, -limit), limit).astype(kind)


def setup_inputs(seed: int = 0) -> dict:
    seeds = jax.random.split(jax.random.key(seed), 5)
    return {
        "phase": jnp.clip(jax.random.uniform(seeds[0], (ROWS, COLUMNS), jnp.float32, -3.140625, 3.140625), -3.140625, 3.140625),
        "target": with_ends((jax.random.randint(seeds[1], (ROWS, COLUMNS), 0, 2) < 1).astype(jnp.int32), jax.random.fold_in(seeds[1], 1), 0, 1),
        "kernels": centred(seeds[2], (2, KERNELS, SUPPORT, SUPPORT), (SUPPORT * SUPPORT) ** -0.5, 0.046875, ((1, 4),), jnp.float32),
        "weights": jnp.clip(jnp.exp(math.log(0.25) - 3.218876 * jax.random.uniform(seeds[3], (KERNELS,), jnp.float32) ** block_levels(seeds[3], (KERNELS,), ((0, 4),), -0.2, 0.2)), 0.01, 0.25),
    }


STEEP = 2.5
LEVEL = 2.0


def reference(phase, target, kernels, weights):
    size_rows = ROWS + 2 * HALF
    size_cols = COLUMNS + 2 * HALF
    transmission = jnp.cos(phase) + 1j * jnp.sin(phase)
    field_hat = jnp.fft.fft2(jnp.pad(transmission, ((0, 2 * HALF), (0, 2 * HALF))))

    def response(index):
        kernel = kernels[0, index] + 1j * kernels[1, index]
        return jnp.fft.fft2(kernel, s=(size_rows, size_cols))

    def field_of(index):
        full = jnp.fft.ifft2(response(index) * field_hat)
        return full[HALF:HALF + ROWS, HALF:HALF + COLUMNS]

    def intensity_step(total, index):
        near = field_of(index)
        return total + weights[index] * (near.real * near.real + near.imag * near.imag), None

    intensity, _ = lax.scan(intensity_step, jnp.zeros((ROWS, COLUMNS), dtype=phase.dtype), jnp.arange(KERNELS))
    resist = jax.nn.sigmoid(STEEP * (intensity - LEVEL))
    slope = 2.0 * STEEP * (resist - target.astype(resist.dtype)) * resist * (1.0 - resist)

    def adjoint_step(total, index):
        spectrum = response(index)
        near = jnp.fft.ifft2(spectrum * field_hat)[HALF:HALF + ROWS, HALF:HALF + COLUMNS]
        pulled = 2.0 * weights[index] * slope * near
        pulled_hat = jnp.fft.fft2(pulled, s=(size_rows, size_cols))
        return total + jnp.conj(spectrum) * pulled_hat, None

    summed_hat, _ = lax.scan(adjoint_step, jnp.zeros_like(field_hat), jnp.arange(KERNELS))
    back = jnp.roll(jnp.fft.ifft2(summed_hat), (HALF, HALF), axis=(0, 1))[:ROWS, :COLUMNS]
    grad_phase = back.imag * jnp.cos(phase) - back.real * jnp.sin(phase)
    return resist, grad_phase
```

```python
import functools

import jax
import jax.numpy as jnp
import ml_dtypes
import numpy as np
from jax import lax
from jax.experimental import pallas as pl
from jax.experimental.pallas import tpu as pltpu
from jax.sharding import PartitionSpec as P

STEEP = 2.5
LEVEL = 2.0
N = 128
H = 64
F32 = jnp.float32
BF16 = jnp.bfloat16
MESH = pl.DeviceIdType.MESH


def tables():
    x = np.arange(N)[:, None]
    k = np.arange(N)[None, :]
    parts = []
    for parity in (0, 1):
        angle = -2.0 * np.pi / (2 * N) * ((2 * k + parity) * x % (2 * N))
        c, s = np.cos(angle), np.sin(angle)
        parts.append(np.block([[c, s], [-s, c]]))
    full = np.concatenate(parts, axis=1)
    high = full.astype(ml_dtypes.bfloat16)
    low = (full - high.astype(np.float64)).astype(ml_dtypes.bfloat16)
    return high, low, np.ascontiguousarray(high.T), np.ascontiguousarray(low.T)


def split(x):
    high = x.astype(BF16)
    return high, (x - high.astype(F32)).astype(BF16)


def dot(a, b):
    return jnp.dot(a, b, preferred_element_type=F32)


def right(x, high, low):
    xh, xl = split(x)
    return dot(xh, high) + dot(xl, high) + dot(xh, low)


def left(high, low, x):
    xh, xl = split(x)
    return dot(high, xh) + dot(high, xl) + dot(low, xh)


def sincos(x):
    turn = jnp.floor(x * (2.0 / np.pi) + 0.5)
    r = x - turn * 1.5707855224609375
    r = r - turn * 1.0804273188e-05
    q = turn.astype(jnp.int32)
    z = r * r
    s = r + r * z * (-1.6666654611e-1 + z * (8.3321608736e-3 + z * -1.9515295891e-4))
    c = 1.0 - 0.5 * z + z * z * (
        4.166664568298827e-2 + z * (-1.388731625493765e-3 + z * 2.443315711809948e-5)
    )
    swap = (q & 1) != 0
    sin = jnp.where(swap, c, s)
    cos = jnp.where(swap, s, c)
    sin = jnp.where((q & 2) != 0, -sin, sin)
    cos = jnp.where(((q + 1) & 2) != 0, -cos, cos)
    return sin, cos


def cat(parts, axis):
    return jnp.concatenate(parts, axis=axis)


def kernel(
    space, groups,
    phase_ref, target_ref, kern_ref, weight_ref, fch, fcl, frh, frl,
    resist_ref, grad_ref,
    halo_out, halo_in, trig, strip, resp, spec, field, inten, inten_in, slope,
    acc, back, gsend, gin, rim_out, rim_in,
    halo_s, halo_r, inten_s, inten_r, slope_s, slope_r, grad_s, grad_r, rim_s, rim_r,
):
    rows = phase_ref.shape[0]
    blocks = rows // N
    kernels = kern_ref.shape[1]
    half = rows // 2
    my_s = lax.axis_index("space")
    my_k = lax.axis_index("kern")
    nxt = (lax.rem(my_s + 1, space), my_k)
    prv = (lax.rem(my_s + space - 1, space), my_k)

    def peer(d):
        return lax.rem(my_k + d, groups)

    barrier = pltpu.get_barrier_semaphore()
    for device in [nxt, prv] + [(my_s, peer(d)) for d in range(1, groups)]:
        pl.semaphore_signal(barrier, inc=1, device_id=device, device_id_type=MESH)
    pl.semaphore_wait(barrier, 1 + groups)

    lane = lax.broadcasted_iota(jnp.int32, (8, N), 1)[:1]

    def pack(upper, lower):
        turned = pltpu.roll(lower, H, 1)
        return jnp.where(lane < H, upper, turned), jnp.where(lane < H, turned, upper)

    def unpack(low_side, high_side):
        upper = jnp.where(lane < H, low_side, high_side)
        return upper, pltpu.roll(jnp.where(lane < H, high_side, low_side), H, 1)

    def remote(src, dst, ssem, rsem, device):
        return pltpu.make_async_remote_copy(
            src_ref=src, dst_ref=dst, send_sem=ssem, recv_sem=rsem,
            device_id=device, device_id_type=MESH,
        )

    to_prev, to_next = pack(phase_ref[:half], phase_ref[half:])
    halo_out[0] = to_prev
    halo_out[1] = to_next
    halo = [
        remote(halo_out.at[0], halo_in.at[0], halo_s.at[0], halo_r.at[0], prv),
        remote(halo_out.at[1], halo_in.at[1], halo_s.at[1], halo_r.at[1], nxt),
    ]
    for copy in halo:
        copy.start()

    zero = jnp.zeros((H, 2 * N), F32)
    for part in range(2):
        strip[part, 0:H] = zero
        strip[part, H + rows : 2 * H + rows] = zero

    def own_trig(b, carry):
        r = pl.ds(pl.multiple_of(b * N, N), N)
        sin, cos = sincos(phase_ref[r])
        trig[0, r] = cos
        trig[1, r] = sin
        return carry

    lax.fori_loop(0, blocks, own_trig, 0)

    row256 = lax.broadcasted_iota(jnp.int32, (N, 2 * N), 0)

    def respond(n, carry):
        even, odd = [], []
        for part in range(2):
            main = kern_ref[part, n, 0:N, 0:N]
            last = jnp.broadcast_to(kern_ref[part, n, N : N + 1, 0:N], (8, N))
            edge = kern_ref[part, n, 0:N, N : N + 1]
            corner = jnp.broadcast_to(kern_ref[part, n, N : N + 1, N : N + 1], (8, 1))
            turned = pltpu.roll(cat([main, last], 0) * 2.0**-16, H, 1)
            extra = jnp.where(lane == H, cat([edge, corner], 0) * 2.0**-16, 0.0)
            even.append(turned + extra)
            odd.append(jnp.where(lane < H, turned, -turned) + extra)
        ge = right(cat(even, 1), fch[:, : 2 * N], fcl[:, : 2 * N])
        go = right(cat(odd, 1), fch[:, 2 * N :], fcl[:, 2 * N :])
        even, odd = [], []
        for c in (slice(0, N), slice(N, 2 * N)):
            g = cat([ge[:, c], go[:, c]], 1)
            extra = jnp.where(row256 == H, g[N : N + 1], 0.0)
            even.append(cat([g[H:N], g[0:H]], 0) + extra)
            odd.append(cat([g[H:N], -g[0:H]], 0) + extra)
        resp[n, : 2 * N] = left(frh[: 2 * N], frl[: 2 * N], cat(even, 0))
        resp[n, 2 * N :] = left(frh[2 * N :], frl[2 * N :], cat(odd, 0))
        return carry

    lax.fori_loop(0, kernels, respond, 0)

    for copy in halo:
        copy.wait_recv()
    no_prev = my_s == 0
    no_next = my_s == space - 1
    outside = jnp.where(
        lane < H, jnp.where(no_next, 0.0, 1.0), jnp.where(no_prev, 0.0, 1.0)
    ).astype(F32)
    upper, lower = unpack(halo_in[0], halo_in[1])
    trig[2, :half] = upper
    trig[2, half:] = lower

    def mask_cols(b, carry):
        r = pl.ds(pl.multiple_of(b * N, N), N)
        sin, cos = sincos(trig[2, r])
        sin = sin * outside
        cos = cos * outside
        trig[2, r] = cos
        trig[3, r] = sin
        cu, su = trig[0, r], trig[1, r]
        se = right(cat([cu + cos, su + sin], 1), fch[:, : 2 * N], fcl[:, : 2 * N])
        so = right(cat([cu - cos, su - sin], 1), fch[:, 2 * N :], fcl[:, 2 * N :])
        q = pl.ds(pl.multiple_of(b * N + H, H), N)
        strip[0, q] = cat([se[:, :N], so[:, :N]], 1)
        strip[1, q] = cat([se[:, N:], so[:, N:]], 1)
        return carry

    lax.fori_loop(0, blocks, mask_cols, 0)

    def mask_rows(b, carry):
        even, odd = [], []
        for part in range(2):
            u = strip[part, pl.ds(pl.multiple_of(b * N + H, H), N)]
            after = strip[part, pl.ds(pl.multiple_of(b * N + H + N, H), H)]
            before = strip[part, pl.ds(pl.multiple_of(b * N, H), H)]
            around = cat([after, before], 0)
            even.append(u + around)
            odd.append(u - around)
        spec[b, : 2 * N] = left(frh[: 2 * N], frl[: 2 * N], cat(even, 0))
        spec[b, 2 * N :] = left(frh[2 * N :], frl[2 * N :], cat(odd, 0))
        return carry

    lax.fori_loop(0, blocks, mask_rows, 0)

    def inten_copy(b, source):
        return remote(
            inten.at[b], inten_in.at[source], inten_s.at[b], inten_r.at[source], (my_s, b)
        )

    def slope_copy(d, owner):
        return remote(
            slope.at[owner], slope.at[owner], slope_s.at[d], slope_r.at[owner], (my_s, peer(d))
        )

    def settle():
        total = inten[my_k]
        for d in range(1, groups):
            inten_copy(my_k, peer(d)).wait_recv()
        for d in range(1, groups):
            total = total + inten_in[peer(d)]
        resist = 1.0 / (1.0 + jnp.exp(-STEEP * (total - LEVEL)))
        resist_ref[...] = resist
        want = target_ref[pl.ds(pl.multiple_of(my_k * N, N), N)].astype(F32)
        slope[my_k] = 2.0 * STEEP * (resist - want) * resist * (1.0 - resist)
        for d in range(1, groups):
            slope_copy(d, my_k).start()

    def fields(b, carry):
        inten[b] = jnp.zeros((N, N), F32)

        def one(n, carry):
            parts = []
            for p in range(2):
                rr = resp[n, 2 * N * p : 2 * N * p + N]
                ri = resp[n, 2 * N * p + N : 2 * N * (p + 1)]
                sr = spec[b, 2 * N * p : 2 * N * p + N]
                si = spec[b, 2 * N * p + N : 2 * N * (p + 1)]
                parts += [rr * sr - ri * si, rr * si + ri * sr]
            z = left(fch[...], fcl[...], cat(parts, 0))
            z = cat([z[:N, :N], z[N:, :N], z[:N, N:], z[N:, N:]], 1)
            f = right(z, frh[...], frl[...])
            field[b, n] = f
            inten[b] += weight_ref[n] * (f[:, :N] * f[:, :N] + f[:, N:] * f[:, N:])
            return carry

        lax.fori_loop(0, kernels, one, 0)

        @pl.when(my_k != b)
        def _():
            inten_copy(b, my_k).start()

        @pl.when(my_k == b - 1)
        def _():
            settle()

        return carry

    lax.fori_loop(0, blocks, fields, 0)

    @pl.when(my_k == groups - 1)
    def _():
        settle()

    for part in range(2):
        back[part] = jnp.zeros((rows + 2 * H, 2 * N), F32)

    def grad_copy(b, source):
        return remote(gsend.at[b], gin.at[source], grad_s.at[b], grad_r.at[source], (my_s, b))

    def finish(b):
        r = pl.ds(pl.multiple_of(b * N, N), N)
        q = pl.ds(pl.multiple_of(b * N + H, H), N)
        br, bi = back[0, q], back[1, q]
        e = right(cat([br[:, :N], bi[:, :N]], 1), frh[: 2 * N], frl[: 2 * N])
        o = right(cat([br[:, N:], bi[:, N:]], 1), frh[2 * N :], frl[2 * N :])
        u = e + o
        v = e - o
        gsend[b, :, :N] = u[:, N:] * trig[0, r] - u[:, :N] * trig[1, r]
        gsend[b, :, N:] = v[:, N:] * trig[2, r] - v[:, :N] * trig[3, r]

        @pl.when(my_k != b)
        def _():
            grad_copy(b, my_k).start()

    def pulls(b, carry):
        @pl.when(my_k != b)
        def _():
            slope_copy(1, b).wait_recv()

        acc[...] = jnp.zeros((4 * N, 2 * N), F32)

        def one(n, carry):
            factor = 2.0 * weight_ref[n] * slope[b]
            f = field[b, n]
            y = right(
                cat([factor * f[:, :N], factor * f[:, N:]], 1), fch[...], fcl[...]
            )
            x = cat(
                [
                    cat([y[:, :N], y[:, 2 * N : 3 * N]], 1),
                    cat([y[:, N : 2 * N], y[:, 3 * N :]], 1),
                ],
                0,
            )
            v = left(frh[...], frl[...], x)
            for p in range(2):
                low = slice(2 * N * p, 2 * N * p + N)
                high = slice(2 * N * p + N, 2 * N * (p + 1))
                rr, ri = resp[n, low], resp[n, high]
                vr, vi = v[low], v[high]
                acc[low] += rr * vr + ri * vi
                acc[high] += rr * vi - ri * vr
            return carry

        lax.fori_loop(0, kernels, one, 0)
        e = left(fch[:, : 2 * N], fcl[:, : 2 * N], acc[: 2 * N])
        o = left(fch[:, 2 * N :], fcl[:, 2 * N :], acc[2 * N :])
        u = e + o
        v = e - o
        for part in range(2):
            p = slice(N * part, N * (part + 1))
            back[part, pl.ds(pl.multiple_of(b * N + H, H), N)] += u[p]
            back[part, pl.ds(pl.multiple_of(b * N + H + N, H), H)] += v[p][:H]
            back[part, pl.ds(pl.multiple_of(b * N, H), H)] += v[p][H:]

        @pl.when(b > 0)
        def _():
            finish(b - 1)

        return carry

    lax.fori_loop(0, blocks, pulls, 0)
    finish(blocks - 1)

    total = gsend[my_k]
    for d in range(1, groups):
        grad_copy(my_k, peer(d)).wait_recv()
    for d in range(1, groups):
        total = total + gin[peer(d)]
    to_next, to_prev = pack(total[:H, N:], total[H:, N:])
    rim_out[0] = to_next
    rim_out[1] = to_prev
    rim = [
        remote(rim_out.at[0], rim_in.at[0], rim_s.at[0], rim_r.at[0], nxt),
        remote(rim_out.at[1], rim_in.at[1], rim_s.at[1], rim_r.at[1], prv),
    ]
    for copy in rim:
        copy.start()
    for copy in rim:
        copy.wait_recv()
    upper, lower = unpack(rim_in[0], rim_in[1])
    inside = jnp.where(
        lane < H, jnp.where(no_prev, 0.0, 1.0), jnp.where(no_next, 0.0, 1.0)
    ).astype(F32)
    grad_ref[:H] = total[:H, :N] + upper * inside
    grad_ref[H:] = total[H:, :N] + lower * inside

    for copy in halo + rim:
        copy.wait_send()
    for d in range(1, groups):
        slope_copy(d, my_k).wait_send()
        inten_copy(peer(d), my_k).wait_send()
        grad_copy(peer(d), my_k).wait_send()


def body(space, groups, phase, target, kernels, weights):
    rows, cols = phase.shape
    blocks = rows // N
    count = kernels.shape[1]
    consts = [jnp.asarray(t) for t in tables()]
    vmem = pl.BlockSpec(memory_space=pltpu.VMEM)
    dma = pltpu.SemaphoreType.DMA
    return pl.pallas_call(
        functools.partial(kernel, space, groups),
        out_shape=[jax.ShapeDtypeStruct((N, cols), F32)] * 2,
        in_specs=[vmem, vmem, vmem, pl.BlockSpec(memory_space=pltpu.SMEM)] + [vmem] * 4,
        out_specs=[vmem, vmem],
        scratch_shapes=[
            pltpu.VMEM((2, rows // 2, N), F32),
            pltpu.VMEM((2, rows // 2, N), F32),
            pltpu.VMEM((4, rows, N), F32),
            pltpu.VMEM((2, rows + 2 * H, 2 * N), F32),
            pltpu.VMEM((count, 4 * N, 2 * N), F32),
            pltpu.VMEM((blocks, 4 * N, 2 * N), F32),
            pltpu.VMEM((blocks, count, N, 2 * N), F32),
            pltpu.VMEM((blocks, N, N), F32),
            pltpu.VMEM((groups, N, N), F32),
            pltpu.VMEM((blocks, N, N), F32),
            pltpu.VMEM((4 * N, 2 * N), F32),
            pltpu.VMEM((2, rows + 2 * H, 2 * N), F32),
            pltpu.VMEM((blocks, N, 2 * N), F32),
            pltpu.VMEM((groups, N, 2 * N), F32),
            pltpu.VMEM((2, H, N), F32),
            pltpu.VMEM((2, H, N), F32),
            dma((2,)), dma((2,)),
            dma((blocks,)), dma((groups,)),
            dma((groups,)), dma((blocks,)),
            dma((blocks,)), dma((groups,)),
            dma((2,)), dma((2,)),
        ],
        compiler_params=pltpu.CompilerParams(
            collective_id=0, has_side_effects=True, vmem_limit_bytes=40 * 2**20
        ),
        cost_estimate=pl.CostEstimate(
            flops=14 * 10**9, bytes_accessed=4 * 10**6, transcendentals=0
        ),
        name="hopkins",
    )(phase, target, kernels, weights, *consts)


def solution(mesh):
    placed = (P(None, "space"), P(None, "space"), P(None, "kern", None, None), P("kern"))
    return jax.shard_map(
        functools.partial(body, mesh.shape["space"], mesh.shape["kern"]),
        mesh=mesh,
        in_specs=placed,
        out_specs=(P("kern", "space"), P("kern", "space")),
        check_vma=False,
    )
```

```python
import functools

import jax
import jax.numpy as jnp
import ml_dtypes
import numpy as np
from jax import lax
from jax.experimental import pallas as pl
from jax.experimental.pallas import tpu as pltpu
from jax.sharding import PartitionSpec as P

STEEP = 2.5
LEVEL = 2.0
N = 128
H = 64
F32 = jnp.float32
BF16 = jnp.bfloat16
MESH = pl.DeviceIdType.MESH


def tables():
    x = np.arange(N)[:, None]
    k = np.arange(N)[None, :]
    parts = []
    for parity in (0, 1):
        angle = -2.0 * np.pi / (2 * N) * ((2 * k + parity) * x % (2 * N))
        c, s = np.cos(angle), np.sin(angle)
        parts.append(np.block([[c, s], [-s, c]]))
    full = np.concatenate(parts, axis=1)
    high = full.astype(ml_dtypes.bfloat16)
    low = (full - high.astype(np.float64)).astype(ml_dtypes.bfloat16)
    return high, low, np.ascontiguousarray(high.T), np.ascontiguousarray(low.T)


def cat(parts, axis):
    return jnp.concatenate(parts, axis=axis)


def split(x):
    high = x.astype(BF16)
    return high, (x - high.astype(F32)).astype(BF16)


def dot(a, b):
    return jnp.dot(a, b, preferred_element_type=F32)


def right(x, high, low):
    xh, xl = split(x)
    return dot(cat([xh, xl, xh], 1), cat([high, high, low], 0))


def left(high, low, x):
    xh, xl = split(x)
    return dot(cat([high, high, low], 1), cat([xh, xl, xh], 0))


def sincos(x):
    turn = jnp.floor(x * (2.0 / np.pi) + 0.5)
    r = x - turn * 1.5707855224609375
    r = r - turn * 1.0804273188e-05
    q = turn.astype(jnp.int32)
    z = r * r
    s = r + r * z * (-1.6666654611e-1 + z * (8.3321608736e-3 + z * -1.9515295891e-4))
    c = 1.0 - 0.5 * z + z * z * (
        4.166664568298827e-2 + z * (-1.388731625493765e-3 + z * 2.443315711809948e-5)
    )
    swap = (q & 1) != 0
    sin = jnp.where(swap, c, s)
    cos = jnp.where(swap, s, c)
    sin = jnp.where((q & 2) != 0, -sin, sin)
    cos = jnp.where(((q + 1) & 2) != 0, -cos, cos)
    return sin, cos


def flip(index, step):
    return index + step - 2 * step * lax.rem(index // step, 2)


def kernel(
    space, groups, far,
    phase_ref, target_ref, kern_ref, weight_ref, fch, fcl, frh, frl,
    resist_ref, grad_ref,
    window, halo_out, halo_in, trig, raw, resp, spec, field, acc, yield_, gout, pout, rin,
    halo_s, halo_r, kern_s, kern_r, rim_s, rim_r,
):
    rows = phase_ref.shape[0]
    count = kern_ref.shape[1]
    tall = N + 8
    my_s = lax.axis_index("space")
    my_k = lax.axis_index("kern")
    s_next = lax.rem(my_s + 1, space)
    s_prev = lax.rem(my_s + space - 1, space)
    k_next = lax.rem(my_k + 1, groups)
    k_prev = lax.rem(my_k + groups - 1, groups)
    sibling = (my_s, flip(my_k, 1))
    across = (my_s, flip(my_k, 2))
    around = (flip(my_s, far), flip(my_k, 2))

    barrier = pltpu.get_barrier_semaphore()
    greeted = [
        (s_next, my_k), (s_prev, my_k), sibling, across, (my_s, flip(flip(my_k, 1), 2)), around,
        (s_next, k_next), (s_next, k_prev), (s_prev, k_next), (s_prev, k_prev),
    ]
    for device in greeted:
        pl.semaphore_signal(barrier, inc=1, device_id=device, device_id_type=MESH)

    lane = lax.broadcasted_iota(jnp.int32, (8, N), 1)[:1]

    def pack(upper, lower):
        turned = pltpu.roll(lower, H, 1)
        return jnp.where(lane < H, upper, turned), jnp.where(lane < H, turned, upper)

    def unpack(low_side, high_side):
        upper = jnp.where(lane < H, low_side, high_side)
        return upper, pltpu.roll(jnp.where(lane < H, high_side, low_side), H, 1)

    def remote(src, dst, ssem, rsem, device):
        return pltpu.make_async_remote_copy(
            src_ref=src, dst_ref=dst, send_sem=ssem, recv_sem=rsem,
            device_id=device, device_id_type=MESH,
        )

    own = pl.multiple_of(my_k * N, N)
    after = pl.multiple_of(jnp.minimum(own + N, rows - H), H)
    before = pl.multiple_of(jnp.maximum(own - H, 0), H)
    window[0:N] = phase_ref[pl.ds(own, N)]
    window[N : N + H] = phase_ref[pl.ds(after, H)]
    window[N + H :] = phase_ref[pl.ds(before, H)]
    halo_out[0], halo_out[1] = pack(window[:N], window[N:])
    halo = [
        remote(halo_out.at[0], halo_in.at[0], halo_s.at[0], halo_r.at[0], (s_prev, my_k)),
        remote(halo_out.at[1], halo_in.at[1], halo_s.at[1], halo_r.at[1], (s_next, my_k)),
    ]

    gains = [
        jnp.sqrt(jnp.zeros((1, N), F32) + weight_ref[n]) * 2.0**-16 for n in range(count)
    ]
    for part in range(2):
        edges = jnp.zeros((8, N), F32)
        for n in range(count):
            gain = gains[n]
            raw[my_k, part, tall * n : tall * n + N] = (
                pltpu.roll(kern_ref[part, n, 0:N, 0:N], H, 1) * gain
            )
            last = jnp.broadcast_to(kern_ref[part, n, N : N + 1, 0:N], (8, N))
            raw[my_k, part, tall * n + N : tall * (n + 1)] = pltpu.roll(last, H, 1) * gain
            for g in range(N // 8 + 1):
                end = 8 * g + 8 if g < N // 8 else N + 1
                column = kern_ref[part, n, 8 * g : end, N : N + 1]
                edges = jnp.where(lane == count * g + n, column * gain, edges)
        raw[my_k, part, tall * count :] = edges

    pl.semaphore_wait(barrier, len(greeted))
    for copy in halo:
        copy.start()

    theirs = flip(my_k, 2)
    to_sibling = remote(raw.at[my_k], raw.at[my_k], kern_s.at[0], kern_r.at[0], sibling)
    to_across = remote(
        raw.at[my_k, 0], raw.at[my_k, 0], kern_s.at[1], kern_r.at[1], across
    )
    to_around = remote(
        raw.at[my_k, 1], raw.at[my_k, 1], kern_s.at[2], kern_r.at[2], around
    )
    onward = remote(raw.at[theirs], raw.at[theirs], kern_s.at[3], kern_r.at[3], sibling)
    to_across.start()
    to_around.start()
    to_sibling.start()

    sin, cos = sincos(window[...])
    row = lax.broadcasted_iota(jnp.int32, (2 * N, N), 0)
    keep = jnp.where(row < N, 1.0, 0.0)
    keep = jnp.where((row >= N) & (row < N + H) & (my_k < groups - 1), 1.0, keep)
    keep = jnp.where((row >= N + H) & (my_k > 0), 1.0, keep)
    trig[0] = cos * keep
    trig[1] = sin * keep

    def owner(j):
        low = jnp.where(lax.rem(j, 2) == 1, flip(my_k, 1), my_k)
        return jnp.where(j >= 2, flip(low, 2), low)

    def respond_cols(j):
        o = owner(j)
        even, odd = [], []
        edges = [raw[o, part, tall * count :] for part in range(2)]
        for n in range(count):
            pair = [[], []]
            for part in range(2):
                turned = raw[o, part, tall * n : tall * (n + 1)]
                extra = cat(
                    [
                        jnp.where(
                            lane == H, edges[part][:, count * g + n : count * g + n + 1], 0.0
                        )
                        for g in range(N // 8 + 1)
                    ],
                    0,
                )
                pair[0].append(turned + extra)
                pair[1].append(jnp.where(lane < H, turned, -turned) + extra)
            even.append(cat(pair[0], 1))
            odd.append(cat(pair[1], 1))
        return (
            right(cat(even, 0), fch[:, : 2 * N], fcl[:, : 2 * N]),
            right(cat(odd, 0), fch[:, 2 * N :], fcl[:, 2 * N :]),
        )

    def respond_rows(j, columns):
        o = owner(j)
        ge, go = columns
        row = lax.broadcasted_iota(jnp.int32, (N, 2 * N), 0)
        even, odd = [], []
        for n in range(count):
            pair = [[], []]
            at = slice(tall * n, tall * (n + 1))
            for c in (slice(0, N), slice(N, 2 * N)):
                g = cat([ge[at, c], go[at, c]], 1)
                extra = jnp.where(row == H, g[N : N + 1], 0.0)
                pair[0].append(cat([g[H:N], g[0:H]], 0) + extra)
                pair[1].append(cat([g[H:N], -g[0:H]], 0) + extra)
            even.append(cat(pair[0], 0))
            odd.append(cat(pair[1], 0))
        for p, x in enumerate((even, odd)):
            half = slice(2 * N * p, 2 * N * (p + 1))
            r = left(frh[half], frl[half], cat(x, 1))
            for n in range(count):
                resp[o, n, half] = r[:, 2 * N * n : 2 * N * (n + 1)]

    def field_rows(j):
        o = owner(j)
        xs = []
        for n in range(count):
            parts = []
            for p in range(2):
                low = slice(2 * N * p, 2 * N * p + N)
                high = slice(2 * N * p + N, 2 * N * (p + 1))
                rr, ri = resp[o, n, low], resp[o, n, high]
                sr, si = spec[low], spec[high]
                parts += [rr * sr - ri * si, rr * si + ri * sr]
            xs.append(cat(parts, 0))
        return left(fch[...], fcl[...], cat(xs, 1))

    def field_cols(j, z):
        o = owner(j)
        zs = []
        for n in range(count):
            q = z[:, 2 * N * n : 2 * N * (n + 1)]
            zs.append(cat([q[:N, :N], q[N:, :N], q[:N, N:], q[N:, N:]], 1))
        f = right(cat(zs, 0), frh[...], frl[...])
        field[o] = f
        q = f * f
        total = None
        for n in range(count):
            g = q[N * n : N * (n + 1)]
            term = g[:, :N] + g[:, N:]
            total = term if total is None else total + term
        return total

    respond_rows(0, respond_cols(0))

    for copy in halo:
        copy.wait_recv()
    first, last = my_s == 0, my_s == space - 1
    upper, lower = unpack(halo_in[0], halo_in[1])
    sin, cos = sincos(cat([upper, lower], 0))
    keep = jnp.where(lane < H, jnp.where(last, 0.0, 1.0), jnp.where(first, 0.0, 1.0)) * keep
    cos = cos * keep
    sin = sin * keep
    trig[2] = cos
    trig[3] = sin
    se = right(
        cat([trig[0] + cos, trig[1] + sin], 1), fch[:, : 2 * N], fcl[:, : 2 * N]
    )
    so = right(
        cat([trig[0] - cos, trig[1] - sin], 1), fch[:, 2 * N :], fcl[:, 2 * N :]
    )
    even, odd = [], []
    for c in (slice(0, N), slice(N, 2 * N)):
        g = cat([se[:, c], so[:, c]], 1)
        even.append(g[:N] + g[N:])
        odd.append(g[:N] - g[N:])
    spec[: 2 * N] = left(frh[: 2 * N], frl[: 2 * N], cat(even, 0))
    spec[2 * N :] = left(frh[2 * N :], frl[2 * N :], cat(odd, 0))

    def fields(j, total):
        @pl.when(j == 0)
        def _():
            to_sibling.wait_recv()

        @pl.when(j == 1)
        def _():
            to_across.wait_recv()
            to_around.wait_recv()
            onward.start()

        @pl.when(j == 2)
        def _():
            onward.wait_recv()

        columns = respond_cols(j + 1)
        z = field_rows(j)
        respond_rows(j + 1, columns)
        return total + field_cols(j, z)

    intensity = lax.fori_loop(0, groups - 1, fields, jnp.zeros((N, N), F32))
    intensity = intensity + field_cols(groups - 1, field_rows(groups - 1))

    resist = 1.0 / (1.0 + jnp.exp(-STEEP * (intensity - LEVEL)))
    resist_ref[...] = resist
    want = target_ref[pl.ds(own, N)].astype(F32)
    factor = 4.0 * STEEP * (resist - want) * resist * (1.0 - resist)

    def pull_cols(j):
        o = owner(j)
        xs = []
        for n in range(count):
            f = field[o, N * n : N * (n + 1)]
            xs.append(cat([factor * f[:, :N], factor * f[:, N:]], 1))
        yield_[lax.rem(j, 2)] = right(cat(xs, 0), fch[...], fcl[...])

    def pull_rows(j):
        o = owner(j)
        y = yield_[lax.rem(j, 2)]
        xs = []
        for n in range(count):
            q = y[N * n : N * (n + 1)]
            re = cat([q[:, :N], q[:, 2 * N : 3 * N]], 1)
            im = cat([q[:, N : 2 * N], q[:, 3 * N :]], 1)
            xs.append(cat([re, im], 0))
        v = left(frh[...], frl[...], cat(xs, 1))
        for p in range(2):
            low = slice(2 * N * p, 2 * N * p + N)
            high = slice(2 * N * p + N, 2 * N * (p + 1))
            re, im = acc[low], acc[high]
            for n in range(count):
                rr, ri = resp[o, n, low], resp[o, n, high]
                vr = v[low, 2 * N * n : 2 * N * (n + 1)]
                vi = v[high, 2 * N * n : 2 * N * (n + 1)]
                re = re + (rr * vr + ri * vi)
                im = im + (rr * vi - ri * vr)
            acc[low] = re
            acc[high] = im

    acc[...] = jnp.zeros((4 * N, 2 * N), F32)
    pull_cols(0)

    def pulls(j, carry):
        pull_cols(j + 1)
        pull_rows(j)
        return carry

    lax.fori_loop(0, groups - 1, pulls, 0)
    pull_rows(groups - 1)

    e = left(fch[:, : 2 * N], fcl[:, : 2 * N], acc[: 2 * N])
    o = left(fch[:, 2 * N :], fcl[:, 2 * N :], acc[2 * N :])
    u, v = e + o, e - o
    br = cat([u[:N], v[:N]], 0)
    bi = cat([u[N:], v[N:]], 0)
    e = right(cat([br[:, :N], bi[:, :N]], 1), frh[: 2 * N], frl[: 2 * N])
    o = right(cat([br[:, N:], bi[:, N:]], 1), frh[2 * N :], frl[2 * N :])
    u, v = e + o, e - o
    gout[0] = u[:, N:] * trig[0] - u[:, :N] * trig[1]
    side = v[:, N:] * trig[2] - v[:, :N] * trig[3]
    gout[1] = side
    pout[0], pout[1] = pack(side[:H], side[H:N])
    low_rows, high_rows = pl.ds(N, H), pl.ds(N + H, H)
    routes = [
        (gout.at[0, low_rows], (my_s, k_next)),
        (gout.at[0, high_rows], (my_s, k_prev)),
        (pout.at[0], (s_next, my_k)),
        (pout.at[1], (s_prev, my_k)),
        (gout.at[1, low_rows], (s_next, k_next)),
        (gout.at[1, low_rows], (s_prev, k_next)),
        (gout.at[1, high_rows], (s_next, k_prev)),
        (gout.at[1, high_rows], (s_prev, k_prev)),
    ]
    rims = [
        remote(src, rin.at[i], rim_s.at[i], rim_r.at[i], device)
        for i, (src, device) in enumerate(routes)
    ]
    for copy in rims:
        copy.start()
    for copy in rims:
        copy.wait_recv()
    has_low = jnp.where(lane < H, my_s, space - 1 - my_s) > 0
    upper, lower = unpack(rin[2], rin[3])
    upper = upper + jnp.where(my_k > 0, jnp.where(lane < H, rin[4], rin[5]), 0.0)
    lower = lower + jnp.where(my_k < groups - 1, jnp.where(lane < H, rin[6], rin[7]), 0.0)
    grad_ref[:H] = (
        gout[0, :H] + jnp.where(my_k > 0, rin[0], 0.0) + jnp.where(has_low, upper, 0.0)
    )
    grad_ref[H:] = (
        gout[0, H:N] + jnp.where(my_k < groups - 1, rin[1], 0.0) + jnp.where(has_low, lower, 0.0)
    )
    for copy in halo + rims + [to_sibling, to_across, to_around, onward]:
        copy.wait_send()


def body(space, groups, phase, target, kernels, weights):
    rows, cols = phase.shape
    count = kernels.shape[1]
    far = 8 if space % 16 == 0 else 1
    consts = [jnp.asarray(t) for t in tables()]
    vmem = pl.BlockSpec(memory_space=pltpu.VMEM)
    dma = pltpu.SemaphoreType.DMA
    return pl.pallas_call(
        functools.partial(kernel, space, groups, far),
        out_shape=[jax.ShapeDtypeStruct((N, cols), F32)] * 2,
        in_specs=[vmem, vmem, vmem, pl.BlockSpec(memory_space=pltpu.SMEM)] + [vmem] * 4,
        out_specs=[vmem, vmem],
        scratch_shapes=[
            pltpu.VMEM((2 * N, N), F32),
            pltpu.VMEM((2, N, N), F32),
            pltpu.VMEM((2, N, N), F32),
            pltpu.VMEM((4, 2 * N, N), F32),
            pltpu.VMEM((groups, 2, count * (N + 8) + 8, N), F32),
            pltpu.VMEM((groups, count, 4 * N, 2 * N), F32),
            pltpu.VMEM((4 * N, 2 * N), F32),
            pltpu.VMEM((groups, count * N, 2 * N), F32),
            pltpu.VMEM((4 * N, 2 * N), F32),
            pltpu.VMEM((2, count * N, 4 * N), F32),
            pltpu.VMEM((2, 2 * N, N), F32),
            pltpu.VMEM((2, H, N), F32),
            pltpu.VMEM((8, H, N), F32),
            dma((2,)), dma((2,)),
            dma((4,)), dma((4,)),
            dma((8,)), dma((8,)),
        ],
        compiler_params=pltpu.CompilerParams(
            collective_id=0, has_side_effects=True, vmem_limit_bytes=48 * 2**20
        ),
        cost_estimate=pl.CostEstimate(
            flops=14 * 10**9, bytes_accessed=4 * 10**6, transcendentals=0
        ),
        name="hopkins",
    )(phase, target, kernels, weights, *consts)


def solution(mesh):
    placed = (P(None, "space"), P(None, "space"), P(None, "kern", None, None), P("kern"))
    return jax.shard_map(
        functools.partial(body, mesh.shape["space"], mesh.shape["kern"]),
        mesh=mesh,
        in_specs=placed,
        out_specs=(P("kern", "space"), P("kern", "space")),
        check_vma=False,
    )
```

```python
import functools

import jax
import jax.numpy as jnp
import ml_dtypes
import numpy as np
from jax import lax
from jax.experimental import pallas as pl
from jax.experimental.pallas import tpu as pltpu
from jax.sharding import PartitionSpec as P

STEEP = 2.5
LEVEL = 2.0
N = 128
H = 64
F32 = jnp.float32
BF16 = jnp.bfloat16
MESH = pl.DeviceIdType.MESH


def tables():
    x = np.arange(N)[:, None]
    k = np.arange(N)[None, :]
    parts = []
    for parity in (0, 1):
        angle = -2.0 * np.pi / (2 * N) * ((2 * k + parity) * x % (2 * N))
        c, s = np.cos(angle), np.sin(angle)
        parts.append(np.block([[c, s], [-s, c]]))
    full = np.concatenate(parts, axis=1)
    high = full.astype(ml_dtypes.bfloat16)
    low = (full - high.astype(np.float64)).astype(ml_dtypes.bfloat16)
    return high, low, np.ascontiguousarray(high.T), np.ascontiguousarray(low.T)


def cat(parts, axis):
    return jnp.concatenate(parts, axis=axis)


def split(x):
    high = x.astype(BF16)
    return high, (x - high.astype(F32)).astype(BF16)


def dot(a, b):
    return jnp.dot(a, b, preferred_element_type=F32)


def right(x, high, low):
    xh, xl = split(x)
    return dot(cat([xh, xl, xh], 1), cat([high, high, low], 0))


def left(high, low, x):
    xh, xl = split(x)
    return dot(cat([high, high, low], 1), cat([xh, xl, xh], 0))


def sincos(x):
    turn = jnp.floor(x * (2.0 / np.pi) + 0.5)
    r = x - turn * 1.5707855224609375
    r = r - turn * 1.0804273188e-05
    q = turn.astype(jnp.int32)
    z = r * r
    s = r + r * z * (-1.6666654611e-1 + z * (8.3321608736e-3 + z * -1.9515295891e-4))
    c = 1.0 - 0.5 * z + z * z * (
        4.166664568298827e-2 + z * (-1.388731625493765e-3 + z * 2.443315711809948e-5)
    )
    swap = (q & 1) != 0
    sin = jnp.where(swap, c, s)
    cos = jnp.where(swap, s, c)
    sin = jnp.where((q & 2) != 0, -sin, sin)
    cos = jnp.where(((q + 1) & 2) != 0, -cos, cos)
    return sin, cos


def flip(index, step):
    return index + step - 2 * step * lax.rem(index // step, 2)


def kernel(
    space, groups, far,
    phase_ref, target_ref, kern_ref, weight_ref, fch, fcl, frh, frl,
    resist_ref, grad_ref,
    window, halo_out, halo_in, trig, raw, resp, spec, field, acc, gout, pout, rin,
    halo_s, halo_r, kern_s, kern_r, rim_s, rim_r,
):
    rows = phase_ref.shape[0]
    count = kern_ref.shape[1]
    tall = N + 8
    my_s = lax.axis_index("space")
    my_k = lax.axis_index("kern")
    s_next = lax.rem(my_s + 1, space)
    s_prev = lax.rem(my_s + space - 1, space)
    k_next = lax.rem(my_k + 1, groups)
    k_prev = lax.rem(my_k + groups - 1, groups)
    sibling = (my_s, flip(my_k, 1))
    across = (my_s, flip(my_k, 2))
    around = (flip(my_s, far), flip(my_k, 2))

    mirror = (my_s, flip(flip(my_k, 1), 2))
    has_next, has_prev = my_s < space - 1, my_s > 0
    up, down = my_k < groups - 1, my_k > 0

    barrier = pltpu.get_barrier_semaphore()
    greeted = [
        (sibling, None), (across, None), (around, None), (mirror, up & down),
        ((s_next, my_k), has_next), ((s_prev, my_k), has_prev),
        ((s_next, k_next), has_next & up), ((s_next, k_prev), has_next & down),
        ((s_prev, k_next), has_prev & up), ((s_prev, k_prev), has_prev & down),
    ]

    def when(condition, action):
        if condition is None:
            action()
        else:
            pl.when(condition)(action)

    expected = 0
    for device, condition in greeted:
        when(
            condition,
            functools.partial(
                pl.semaphore_signal, barrier, inc=1, device_id=device, device_id_type=MESH
            ),
        )
        expected = expected + (1 if condition is None else jnp.where(condition, 1, 0))

    lane = lax.broadcasted_iota(jnp.int32, (8, N), 1)[:1]

    def pack(upper, lower):
        turned = pltpu.roll(lower, H, 1)
        return jnp.where(lane < H, upper, turned), jnp.where(lane < H, turned, upper)

    def unpack(low_side, high_side):
        upper = jnp.where(lane < H, low_side, high_side)
        return upper, pltpu.roll(jnp.where(lane < H, high_side, low_side), H, 1)

    def remote(src, dst, ssem, rsem, device):
        return pltpu.make_async_remote_copy(
            src_ref=src, dst_ref=dst, send_sem=ssem, recv_sem=rsem,
            device_id=device, device_id_type=MESH,
        )

    own = pl.multiple_of(my_k * N, N)
    after = pl.multiple_of(jnp.minimum(own + N, rows - H), H)
    before = pl.multiple_of(jnp.maximum(own - H, 0), H)
    window[0:N] = phase_ref[pl.ds(own, N)]
    window[N : N + H] = phase_ref[pl.ds(after, H)]
    window[N + H :] = phase_ref[pl.ds(before, H)]
    halo_out[0], halo_out[1] = pack(window[:N], window[N:])
    halo = [
        remote(halo_out.at[0], halo_in.at[0], halo_s.at[0], halo_r.at[0], (s_prev, my_k)),
        remote(halo_out.at[1], halo_in.at[1], halo_s.at[1], halo_r.at[1], (s_next, my_k)),
    ]

    gains = [
        jnp.sqrt(jnp.zeros((1, N), F32) + weight_ref[n]) * 2.0**-16 for n in range(count)
    ]
    for part in range(2):
        edges = jnp.zeros((8, N), F32)
        for n in range(count):
            gain = gains[n]
            raw[0, part, tall * n : tall * n + N] = (
                pltpu.roll(kern_ref[part, n, 0:N, 0:N], H, 1) * gain
            )
            last = jnp.broadcast_to(kern_ref[part, n, N : N + 1, 0:N], (8, N))
            raw[0, part, tall * n + N : tall * (n + 1)] = pltpu.roll(last, H, 1) * gain
            for g in range(N // 8 + 1):
                end = 8 * g + 8 if g < N // 8 else N + 1
                column = kern_ref[part, n, 8 * g : end, N : N + 1]
                edges = jnp.where(lane == count * g + n, column * gain, edges)
        raw[0, part, tall * count :] = edges

    pl.semaphore_wait(barrier, expected)
    when(has_prev, halo[0].start)
    when(has_next, halo[1].start)

    theirs = flip(my_k, 2)
    to_across = remote(raw.at[0, 0], raw.at[1, 0], kern_s.at[0], kern_r.at[0], across)
    to_around = remote(raw.at[0, 1], raw.at[1, 1], kern_s.at[1], kern_r.at[1], around)
    to_across.start()
    to_around.start()

    def shared(group, parity, index):
        half = resp.at[group, :, pl.ds(2 * N * parity, 2 * N)]
        return remote(half, half, kern_s.at[index], kern_r.at[index], sibling)

    first_group = [shared(my_k, 0, 2), shared(my_k, 1, 3)]
    second_group = [shared(theirs, 0, 4), shared(theirs, 1, 5)]

    sin, cos = sincos(window[...])
    row = lax.broadcasted_iota(jnp.int32, (2 * N, N), 0)
    missing = jnp.where((row >= N) & (row < N + H) & (my_k == groups - 1), 1, 0)
    missing = jnp.where((row >= N + H) & (my_k == 0), 1, missing)
    trig[0] = jnp.where(missing == 0, cos, 0.0)
    trig[1] = jnp.where(missing == 0, sin, 0.0)

    def respond_cols(o):
        even, odd = [], []
        edges = [raw[o, part, tall * count :] for part in range(2)]
        for n in range(count):
            pair = [[], []]
            for part in range(2):
                turned = raw[o, part, tall * n : tall * (n + 1)]
                extra = cat(
                    [
                        jnp.where(
                            lane == H, edges[part][:, count * g + n : count * g + n + 1], 0.0
                        )
                        for g in range(N // 8 + 1)
                    ],
                    0,
                )
                pair[0].append(turned + extra)
                pair[1].append(jnp.where(lane < H, turned, -turned) + extra)
            even.append(cat(pair[0], 1))
            odd.append(cat(pair[1], 1))
        return (
            right(cat(even, 0), fch[:, : 2 * N], fcl[:, : 2 * N]),
            right(cat(odd, 0), fch[:, 2 * N :], fcl[:, 2 * N :]),
        )

    def respond_rows(o, columns, copies):
        ge, go = columns
        row = lax.broadcasted_iota(jnp.int32, (N, 2 * N), 0)
        even, odd = [], []
        for n in range(count):
            pair = [[], []]
            at = slice(tall * n, tall * (n + 1))
            for c in (slice(0, N), slice(N, 2 * N)):
                g = cat([ge[at, c], go[at, c]], 1)
                extra = jnp.where(row == H, g[N : N + 1], 0.0)
                pair[0].append(cat([g[H:N], g[0:H]], 0) + extra)
                pair[1].append(cat([g[H:N], -g[0:H]], 0) + extra)
            even.append(cat(pair[0], 0))
            odd.append(cat(pair[1], 0))
        for p, x in enumerate((even, odd)):
            half = slice(2 * N * p, 2 * N * (p + 1))
            r = left(frh[half], frl[half], cat(x, 1))
            for n in range(count):
                resp[o, n, half] = r[:, 2 * N * n : 2 * N * (n + 1)]
            copies[p].start()

    def members(owners):
        return [(o, n) for o in owners for n in range(count)]

    def field_rows(owners):
        xs = []
        for o, n in members(owners):
            parts = []
            for p in range(2):
                low = slice(2 * N * p, 2 * N * p + N)
                high = slice(2 * N * p + N, 2 * N * (p + 1))
                rr, ri = resp[o, n, low], resp[o, n, high]
                sr, si = spec[low], spec[high]
                parts += [rr * sr - ri * si, rr * si + ri * sr]
            xs.append(cat(parts, 0))
        return left(fch[...], fcl[...], cat(xs, 1))

    def fields(owners):
        z = field_rows(owners)
        zs = []
        for n in range(len(owners) * count):
            q = z[:, 2 * N * n : 2 * N * (n + 1)]
            zs.append(cat([q[:N, :N], q[N:, :N], q[:N, N:], q[N:, N:]], 1))
        f = right(cat(zs, 0), frh[...], frl[...])
        for i, o in enumerate(owners):
            field[o] = f[N * count * i : N * count * (i + 1)]
        q = f * f
        total = None
        for n in range(len(owners) * count):
            g = q[N * n : N * (n + 1)]
            term = g[:, :N] + g[:, N:]
            total = term if total is None else total + term
        return total

    respond_rows(my_k, respond_cols(0), first_group)

    when(has_next, halo[0].wait_recv)
    when(has_prev, halo[1].wait_recv)
    upper, lower = unpack(halo_in[0], halo_in[1])
    sin, cos = sincos(cat([upper, lower], 0))
    inside = jnp.where(lane < H, space - 1 - my_s, my_s) > 0
    cos = jnp.where(inside & (missing == 0), cos, 0.0)
    sin = jnp.where(inside & (missing == 0), sin, 0.0)
    trig[2] = cos
    trig[3] = sin
    se = right(
        cat([trig[0] + cos, trig[1] + sin], 1), fch[:, : 2 * N], fcl[:, : 2 * N]
    )
    so = right(
        cat([trig[0] - cos, trig[1] - sin], 1), fch[:, 2 * N :], fcl[:, 2 * N :]
    )
    even, odd = [], []
    for c in (slice(0, N), slice(N, 2 * N)):
        g = cat([se[:, c], so[:, c]], 1)
        even.append(g[:N] + g[N:])
        odd.append(g[:N] - g[N:])
    spec[: 2 * N] = left(frh[: 2 * N], frl[: 2 * N], cat(even, 0))
    spec[2 * N :] = left(frh[2 * N :], frl[2 * N :], cat(odd, 0))

    kin, theirs_kin = flip(my_k, 1), flip(theirs, 1)
    for copy in first_group:
        copy.wait_recv()
    intensity = fields((my_k, kin))
    to_across.wait_recv()
    to_around.wait_recv()
    respond_rows(theirs, respond_cols(1), second_group)
    intensity = intensity + fields((theirs,))
    for copy in second_group:
        copy.wait_recv()
    intensity = intensity + fields((theirs_kin,))

    resist = 1.0 / (1.0 + jnp.exp(-STEEP * (intensity - LEVEL)))
    resist_ref[...] = resist
    want = target_ref[pl.ds(own, N)].astype(F32)
    factor = 4.0 * STEEP * (resist - want) * resist * (1.0 - resist)

    def pulls(owners):
        xs = []
        for o, n in members(owners):
            f = field[o, N * n : N * (n + 1)]
            xs.append(cat([factor * f[:, :N], factor * f[:, N:]], 1))
        y = right(cat(xs, 0), fch[...], fcl[...])
        xs = []
        for i in range(len(owners) * count):
            q = y[N * i : N * (i + 1)]
            re = cat([q[:, :N], q[:, 2 * N : 3 * N]], 1)
            im = cat([q[:, N : 2 * N], q[:, 3 * N :]], 1)
            xs.append(cat([re, im], 0))
        v = left(frh[...], frl[...], cat(xs, 1))
        for p in range(2):
            low = slice(2 * N * p, 2 * N * p + N)
            high = slice(2 * N * p + N, 2 * N * (p + 1))
            re, im = acc[low], acc[high]
            for i, (o, n) in enumerate(members(owners)):
                rr, ri = resp[o, n, low], resp[o, n, high]
                vr = v[low, 2 * N * i : 2 * N * (i + 1)]
                vi = v[high, 2 * N * i : 2 * N * (i + 1)]
                re = re + (rr * vr + ri * vi)
                im = im + (rr * vi - ri * vr)
            acc[low] = re
            acc[high] = im

    acc[...] = jnp.zeros((4 * N, 2 * N), F32)

    def pull_step(j, carry):
        low = jnp.where(j == 0, my_k, theirs)
        pulls((low, flip(low, 1)))
        return carry

    lax.fori_loop(0, 2, pull_step, 0)

    e = left(fch[:, : 2 * N], fcl[:, : 2 * N], acc[: 2 * N])
    o = left(fch[:, 2 * N :], fcl[:, 2 * N :], acc[2 * N :])
    u, v = e + o, e - o
    br = cat([u[:N], v[:N]], 0)
    bi = cat([u[N:], v[N:]], 0)
    e = right(cat([br[:, :N], bi[:, :N]], 1), frh[: 2 * N], frl[: 2 * N])
    o = right(cat([br[:, N:], bi[:, N:]], 1), frh[2 * N :], frl[2 * N :])
    u, v = e + o, e - o
    gout[0] = u[:, N:] * trig[0] - u[:, :N] * trig[1]
    side = v[:, N:] * trig[2] - v[:, :N] * trig[3]
    gout[1] = side
    pout[0], pout[1] = pack(side[:H], side[H:N])
    low_rows, high_rows = pl.ds(N, H), pl.ds(N + H, H)
    routes = [
        (gout.at[0, low_rows], (my_s, k_next), up, down),
        (gout.at[0, high_rows], (my_s, k_prev), down, up),
        (pout.at[0], (s_next, my_k), has_next, has_prev),
        (pout.at[1], (s_prev, my_k), has_prev, has_next),
        (gout.at[1, low_rows], (s_next, k_next), has_next & up, has_prev & down),
        (gout.at[1, low_rows], (s_prev, k_next), has_prev & up, has_next & down),
        (gout.at[1, high_rows], (s_next, k_prev), has_next & down, has_prev & up),
        (gout.at[1, high_rows], (s_prev, k_prev), has_prev & down, has_next & up),
    ]
    rims = [
        remote(src, rin.at[i], rim_s.at[i], rim_r.at[i], device)
        for i, (src, device, _, _) in enumerate(routes)
    ]
    for i in (4, 5, 6, 7, 2, 3, 0, 1):
        when(routes[i][2], rims[i].start)
    for i in range(8):
        when(routes[i][3], rims[i].wait_recv)
    has_low = jnp.where(lane < H, my_s, space - 1 - my_s) > 0
    upper, lower = unpack(rin[2], rin[3])
    upper = upper + jnp.where(my_k > 0, jnp.where(lane < H, rin[4], rin[5]), 0.0)
    lower = lower + jnp.where(my_k < groups - 1, jnp.where(lane < H, rin[6], rin[7]), 0.0)
    grad_ref[:H] = (
        gout[0, :H] + jnp.where(my_k > 0, rin[0], 0.0) + jnp.where(has_low, upper, 0.0)
    )
    grad_ref[H:] = (
        gout[0, H:N] + jnp.where(my_k < groups - 1, rin[1], 0.0) + jnp.where(has_low, lower, 0.0)
    )
    when(has_prev, halo[0].wait_send)
    when(has_next, halo[1].wait_send)
    for copy in [to_across, to_around] + first_group + second_group:
        copy.wait_send()
    for i in range(8):
        when(routes[i][2], rims[i].wait_send)


def body(space, groups, phase, target, kernels, weights):
    rows, cols = phase.shape
    count = kernels.shape[1]
    far = 8 if space % 16 == 0 else 1
    consts = [jnp.asarray(t) for t in tables()]
    vmem = pl.BlockSpec(memory_space=pltpu.VMEM)
    dma = pltpu.SemaphoreType.DMA
    return pl.pallas_call(
        functools.partial(kernel, space, groups, far),
        out_shape=[jax.ShapeDtypeStruct((N, cols), F32)] * 2,
        in_specs=[vmem, vmem, vmem, pl.BlockSpec(memory_space=pltpu.SMEM)] + [vmem] * 4,
        out_specs=[vmem, vmem],
        scratch_shapes=[
            pltpu.VMEM((2 * N, N), F32),
            pltpu.VMEM((2, N, N), F32),
            pltpu.VMEM((2, N, N), F32),
            pltpu.VMEM((4, 2 * N, N), F32),
            pltpu.VMEM((2, 2, count * (N + 8) + 8, N), F32),
            pltpu.VMEM((groups, count, 4 * N, 2 * N), F32),
            pltpu.VMEM((4 * N, 2 * N), F32),
            pltpu.VMEM((groups, count * N, 2 * N), F32),
            pltpu.VMEM((4 * N, 2 * N), F32),
            pltpu.VMEM((2, 2 * N, N), F32),
            pltpu.VMEM((2, H, N), F32),
            pltpu.VMEM((8, H, N), F32),
            dma((2,)), dma((2,)),
            dma((6,)), dma((6,)),
            dma((8,)), dma((8,)),
        ],
        compiler_params=pltpu.CompilerParams(
            collective_id=0, has_side_effects=True, vmem_limit_bytes=48 * 2**20
        ),
        cost_estimate=pl.CostEstimate(
            flops=14 * 10**9, bytes_accessed=4 * 10**6, transcendentals=0
        ),
        name="hopkins",
    )(phase, target, kernels, weights, *consts)


def solution(mesh):
    placed = (P(None, "space"), P(None, "space"), P(None, "kern", None, None), P("kern"))
    return jax.shard_map(
        functools.partial(body, mesh.shape["space"], mesh.shape["kern"]),
        mesh=mesh,
        in_specs=placed,
        out_specs=(P("kern", "space"), P("kern", "space")),
        check_vma=False,
    )
```

```python
import functools

import jax
import jax.numpy as jnp
import ml_dtypes
import numpy as np
from jax import lax
from jax.experimental import pallas as pl
from jax.experimental.pallas import tpu as pltpu
from jax.sharding import PartitionSpec as P

STEEP = 2.5
LEVEL = 2.0
N = 128
H = 64
F32 = jnp.float32
BF16 = jnp.bfloat16
MESH = pl.DeviceIdType.MESH


def tables():
    x = np.arange(N)[:, None]
    k = np.arange(N)[None, :]
    parts = []
    for parity in (0, 1):
        angle = -2.0 * np.pi / (2 * N) * ((2 * k + parity) * x % (2 * N))
        c, s = np.cos(angle), np.sin(angle)
        parts.append(np.block([[c, s], [-s, c]]))
    full = np.concatenate(parts, axis=1)
    high = full.astype(ml_dtypes.bfloat16)
    low = (full - high.astype(np.float64)).astype(ml_dtypes.bfloat16)
    return high, low, np.ascontiguousarray(high.T), np.ascontiguousarray(low.T)


def cat(parts, axis):
    return jnp.concatenate(parts, axis=axis)


def split(x):
    high = x.astype(BF16)
    return high, (x - high.astype(F32)).astype(BF16)


def dot(a, b):
    return jnp.dot(a, b, preferred_element_type=F32)


def right(x, high, low):
    xh, xl = split(x)
    return dot(cat([xh, xl, xh], 1), cat([high, high, low], 0))


def left(high, low, x):
    xh, xl = split(x)
    return dot(cat([high, high, low], 1), cat([xh, xl, xh], 0))


def sincos(x):
    turn = jnp.floor(x * (2.0 / np.pi) + 0.5)
    r = x - turn * 1.5707855224609375
    r = r - turn * 1.0804273188e-05
    q = turn.astype(jnp.int32)
    z = r * r
    s = r + r * z * (-1.6666654611e-1 + z * (8.3321608736e-3 + z * -1.9515295891e-4))
    c = 1.0 - 0.5 * z + z * z * (
        4.166664568298827e-2 + z * (-1.388731625493765e-3 + z * 2.443315711809948e-5)
    )
    swap = (q & 1) != 0
    sin = jnp.where(swap, c, s)
    cos = jnp.where(swap, s, c)
    sin = jnp.where((q & 2) != 0, -sin, sin)
    cos = jnp.where(((q + 1) & 2) != 0, -cos, cos)
    return sin, cos


def flip(index, step):
    return index + step - 2 * step * lax.rem(index // step, 2)


def kernel(
    space, groups, far,
    phase_hbm, target_hbm, kern_hbm, weight_ref, fch_hbm, fcl_hbm, frh_hbm, frl_hbm,
    resist_ref, grad_ref,
    phase_ref, target_ref, kern_ref, fch, fcl, frh, frl, load_s,
    window, halo_out, halo_in, trig, raw, resp, spec, field, acc, gout, pout, rin,
    halo_s, halo_r, kern_s, kern_r, rim_s, rim_r,
):
    rows = phase_hbm.shape[0]
    count = kern_hbm.shape[2]
    my_k = lax.axis_index("kern")
    own = pl.multiple_of(my_k * N, N)
    pairs = [(phase_hbm, phase_ref)]
    pairs += [
        (kern_hbm.at[part, :, n], kern_ref.at[part, n]) for part in range(2) for n in range(count)
    ]
    pairs += [(fch_hbm, fch), (fcl_hbm, fcl), (frh_hbm, frh), (frl_hbm, frl)]
    pairs += [(target_hbm.at[pl.ds(own, N)], target_ref)]
    loads = [
        pltpu.make_async_copy(src, dst, load_s.at[i]) for i, (src, dst) in enumerate(pairs)
    ]
    for load in loads:
        load.start()
    tall = N + 8
    my_s = lax.axis_index("space")
    s_next = lax.rem(my_s + 1, space)
    s_prev = lax.rem(my_s + space - 1, space)
    k_next = lax.rem(my_k + 1, groups)
    k_prev = lax.rem(my_k + groups - 1, groups)
    sibling = (my_s, flip(my_k, 1))
    across = (my_s, flip(my_k, 2))
    around = (flip(my_s, far), flip(my_k, 2))

    mirror = (my_s, flip(flip(my_k, 1), 2))
    has_next, has_prev = my_s < space - 1, my_s > 0
    up, down = my_k < groups - 1, my_k > 0

    barrier = pltpu.get_barrier_semaphore()
    greeted = [
        (sibling, None), (across, None), (around, None), (mirror, up & down),
        ((s_next, my_k), has_next), ((s_prev, my_k), has_prev),
        ((s_next, k_next), has_next & up), ((s_next, k_prev), has_next & down),
        ((s_prev, k_next), has_prev & up), ((s_prev, k_prev), has_prev & down),
    ]

    def when(condition, action):
        if condition is None:
            action()
        else:
            pl.when(condition)(action)

    expected = 0
    for device, condition in greeted:
        when(
            condition,
            functools.partial(
                pl.semaphore_signal, barrier, inc=1, device_id=device, device_id_type=MESH
            ),
        )
        expected = expected + (1 if condition is None else jnp.where(condition, 1, 0))

    lane = lax.broadcasted_iota(jnp.int32, (8, N), 1)[:1]

    def pack(upper, lower):
        turned = pltpu.roll(lower, H, 1)
        return jnp.where(lane < H, upper, turned), jnp.where(lane < H, turned, upper)

    def unpack(low_side, high_side):
        upper = jnp.where(lane < H, low_side, high_side)
        return upper, pltpu.roll(jnp.where(lane < H, high_side, low_side), H, 1)

    def remote(src, dst, ssem, rsem, device):
        return pltpu.make_async_remote_copy(
            src_ref=src, dst_ref=dst, send_sem=ssem, recv_sem=rsem,
            device_id=device, device_id_type=MESH,
        )

    loads[0].wait()
    after = pl.multiple_of(jnp.minimum(own + N, rows - H), H)
    before = pl.multiple_of(jnp.maximum(own - H, 0), H)
    window[0:N] = phase_ref[pl.ds(own, N)]
    window[N : N + H] = phase_ref[pl.ds(after, H)]
    window[N + H :] = phase_ref[pl.ds(before, H)]
    halo_out[0], halo_out[1] = pack(window[:N], window[N:])
    halo = [
        remote(halo_out.at[0], halo_in.at[0], halo_s.at[0], halo_r.at[0], (s_prev, my_k)),
        remote(halo_out.at[1], halo_in.at[1], halo_s.at[1], halo_r.at[1], (s_next, my_k)),
    ]

    for load in loads[1 : 1 + 2 * count]:
        load.wait()
    gains = [
        jnp.sqrt(jnp.zeros((1, N), F32) + weight_ref[n]) * 2.0**-16 for n in range(count)
    ]
    for part in range(2):
        edges = jnp.zeros((8, N), F32)
        for n in range(count):
            gain = gains[n]
            raw[0, part, tall * n : tall * n + N] = (
                pltpu.roll(kern_ref[part, n, 0:N, 0:N], H, 1) * gain
            )
            last = jnp.broadcast_to(kern_ref[part, n, N : N + 1, 0:N], (8, N))
            raw[0, part, tall * n + N : tall * (n + 1)] = pltpu.roll(last, H, 1) * gain
            for g in range(N // 8 + 1):
                end = 8 * g + 8 if g < N // 8 else N + 1
                column = kern_ref[part, n, 8 * g : end, N : N + 1]
                edges = jnp.where(lane == count * g + n, column * gain, edges)
        raw[0, part, tall * count :] = edges

    pl.semaphore_wait(barrier, expected)
    when(has_prev, halo[0].start)
    when(has_next, halo[1].start)

    theirs = flip(my_k, 2)
    to_across = remote(raw.at[0, 0], raw.at[1, 0], kern_s.at[0], kern_r.at[0], across)
    to_around = remote(raw.at[0, 1], raw.at[1, 1], kern_s.at[1], kern_r.at[1], around)
    to_across.start()
    to_around.start()

    def shared(group, parity, index):
        half = resp.at[group, :, pl.ds(2 * N * parity, 2 * N)]
        return remote(half, half, kern_s.at[index], kern_r.at[index], sibling)

    first_group = [shared(my_k, 0, 2), shared(my_k, 1, 3)]
    second_group = [shared(theirs, 0, 4), shared(theirs, 1, 5)]

    sin, cos = sincos(window[...])
    row = lax.broadcasted_iota(jnp.int32, (2 * N, N), 0)
    missing = jnp.where((row >= N) & (row < N + H) & (my_k == groups - 1), 1, 0)
    missing = jnp.where((row >= N + H) & (my_k == 0), 1, missing)
    trig[0] = jnp.where(missing == 0, cos, 0.0)
    trig[1] = jnp.where(missing == 0, sin, 0.0)

    def respond_cols(o):
        even, odd = [], []
        edges = [raw[o, part, tall * count :] for part in range(2)]
        for n in range(count):
            pair = [[], []]
            for part in range(2):
                turned = raw[o, part, tall * n : tall * (n + 1)]
                extra = cat(
                    [
                        jnp.where(
                            lane == H, edges[part][:, count * g + n : count * g + n + 1], 0.0
                        )
                        for g in range(N // 8 + 1)
                    ],
                    0,
                )
                pair[0].append(turned + extra)
                pair[1].append(jnp.where(lane < H, turned, -turned) + extra)
            even.append(cat(pair[0], 1))
            odd.append(cat(pair[1], 1))
        return (
            right(cat(even, 0), fch[:, : 2 * N], fcl[:, : 2 * N]),
            right(cat(odd, 0), fch[:, 2 * N :], fcl[:, 2 * N :]),
        )

    def respond_rows(o, columns, copies):
        ge, go = columns
        row = lax.broadcasted_iota(jnp.int32, (N, 2 * N), 0)
        even, odd = [], []
        for n in range(count):
            pair = [[], []]
            at = slice(tall * n, tall * (n + 1))
            for c in (slice(0, N), slice(N, 2 * N)):
                g = cat([ge[at, c], go[at, c]], 1)
                extra = jnp.where(row == H, g[N : N + 1], 0.0)
                pair[0].append(cat([g[H:N], g[0:H]], 0) + extra)
                pair[1].append(cat([g[H:N], -g[0:H]], 0) + extra)
            even.append(cat(pair[0], 0))
            odd.append(cat(pair[1], 0))
        for p, x in enumerate((even, odd)):
            half = slice(2 * N * p, 2 * N * (p + 1))
            r = left(frh[half], frl[half], cat(x, 1))
            for n in range(count):
                resp[o, n, half] = r[:, 2 * N * n : 2 * N * (n + 1)]
            copies[p].start()

    def members(owners):
        return [(o, n) for o in owners for n in range(count)]

    def field_rows(owners):
        xs = []
        for o, n in members(owners):
            parts = []
            for p in range(2):
                low = slice(2 * N * p, 2 * N * p + N)
                high = slice(2 * N * p + N, 2 * N * (p + 1))
                rr, ri = resp[o, n, low], resp[o, n, high]
                sr, si = spec[low], spec[high]
                parts += [rr * sr - ri * si, rr * si + ri * sr]
            xs.append(cat(parts, 0))
        return left(fch[...], fcl[...], cat(xs, 1))

    def fields(owners):
        z = field_rows(owners)
        zs = []
        for n in range(len(owners) * count):
            q = z[:, 2 * N * n : 2 * N * (n + 1)]
            zs.append(cat([q[:N, :N], q[N:, :N], q[:N, N:], q[N:, N:]], 1))
        f = right(cat(zs, 0), frh[...], frl[...])
        for i, o in enumerate(owners):
            field[o] = f[N * count * i : N * count * (i + 1)]
        q = f * f
        total = None
        for n in range(len(owners) * count):
            g = q[N * n : N * (n + 1)]
            term = g[:, :N] + g[:, N:]
            total = term if total is None else total + term
        return total

    for load in loads[1 + 2 * count :]:
        load.wait()
    respond_rows(my_k, respond_cols(0), first_group)
    to_across.wait_recv()
    to_around.wait_recv()
    respond_rows(theirs, respond_cols(1), second_group)

    when(has_next, halo[0].wait_recv)
    when(has_prev, halo[1].wait_recv)
    upper, lower = unpack(halo_in[0], halo_in[1])
    sin, cos = sincos(cat([upper, lower], 0))
    inside = jnp.where(lane < H, space - 1 - my_s, my_s) > 0
    cos = jnp.where(inside & (missing == 0), cos, 0.0)
    sin = jnp.where(inside & (missing == 0), sin, 0.0)
    trig[2] = cos
    trig[3] = sin
    se = right(
        cat([trig[0] + cos, trig[1] + sin], 1), fch[:, : 2 * N], fcl[:, : 2 * N]
    )
    so = right(
        cat([trig[0] - cos, trig[1] - sin], 1), fch[:, 2 * N :], fcl[:, 2 * N :]
    )
    even, odd = [], []
    for c in (slice(0, N), slice(N, 2 * N)):
        g = cat([se[:, c], so[:, c]], 1)
        even.append(g[:N] + g[N:])
        odd.append(g[:N] - g[N:])
    spec[: 2 * N] = left(frh[: 2 * N], frl[: 2 * N], cat(even, 0))
    spec[2 * N :] = left(frh[2 * N :], frl[2 * N :], cat(odd, 0))

    kin, theirs_kin = flip(my_k, 1), flip(theirs, 1)
    for copy in first_group:
        copy.wait_recv()
    intensity = fields((my_k, kin))
    intensity = intensity + fields((theirs,))
    for copy in second_group:
        copy.wait_recv()
    intensity = intensity + fields((theirs_kin,))

    resist = 1.0 / (1.0 + jnp.exp(-STEEP * (intensity - LEVEL)))
    resist_ref[...] = resist
    want = target_ref[...].astype(F32)
    factor = 4.0 * STEEP * (resist - want) * resist * (1.0 - resist)

    def pulls(owners):
        xs = []
        for o, n in members(owners):
            f = field[o, N * n : N * (n + 1)]
            xs.append(cat([factor * f[:, :N], factor * f[:, N:]], 1))
        y = right(cat(xs, 0), fch[...], fcl[...])
        xs = []
        for i in range(len(owners) * count):
            q = y[N * i : N * (i + 1)]
            re = cat([q[:, :N], q[:, 2 * N : 3 * N]], 1)
            im = cat([q[:, N : 2 * N], q[:, 3 * N :]], 1)
            xs.append(cat([re, im], 0))
        v = left(frh[...], frl[...], cat(xs, 1))
        for p in range(2):
            low = slice(2 * N * p, 2 * N * p + N)
            high = slice(2 * N * p + N, 2 * N * (p + 1))
            re, im = acc[low], acc[high]
            for i, (o, n) in enumerate(members(owners)):
                rr, ri = resp[o, n, low], resp[o, n, high]
                vr = v[low, 2 * N * i : 2 * N * (i + 1)]
                vi = v[high, 2 * N * i : 2 * N * (i + 1)]
                re = re + (rr * vr + ri * vi)
                im = im + (rr * vi - ri * vr)
            acc[low] = re
            acc[high] = im

    acc[...] = jnp.zeros((4 * N, 2 * N), F32)

    def pull_step(j, carry):
        low = jnp.where(j == 0, my_k, theirs)
        pulls((low, flip(low, 1)))
        return carry

    lax.fori_loop(0, 2, pull_step, 0)

    e = left(fch[:, : 2 * N], fcl[:, : 2 * N], acc[: 2 * N])
    o = left(fch[:, 2 * N :], fcl[:, 2 * N :], acc[2 * N :])
    u, v = e + o, e - o
    br = cat([u[:N], v[:N]], 0)
    bi = cat([u[N:], v[N:]], 0)
    e = right(cat([br[:, :N], bi[:, :N]], 1), frh[: 2 * N], frl[: 2 * N])
    o = right(cat([br[:, N:], bi[:, N:]], 1), frh[2 * N :], frl[2 * N :])
    u, v = e + o, e - o
    gout[0] = u[:, N:] * trig[0] - u[:, :N] * trig[1]
    side = v[:, N:] * trig[2] - v[:, :N] * trig[3]
    gout[1] = side
    pout[0], pout[1] = pack(side[:H], side[H:N])
    low_rows, high_rows = pl.ds(N, H), pl.ds(N + H, H)
    routes = [
        (gout.at[0, low_rows], (my_s, k_next), up, down),
        (gout.at[0, high_rows], (my_s, k_prev), down, up),
        (pout.at[0], (s_next, my_k), has_next, has_prev),
        (pout.at[1], (s_prev, my_k), has_prev, has_next),
        (gout.at[1, low_rows], (s_next, k_next), has_next & up, has_prev & down),
        (gout.at[1, low_rows], (s_prev, k_next), has_prev & up, has_next & down),
        (gout.at[1, high_rows], (s_next, k_prev), has_next & down, has_prev & up),
        (gout.at[1, high_rows], (s_prev, k_prev), has_prev & down, has_next & up),
    ]
    rims = [
        remote(src, rin.at[i], rim_s.at[i], rim_r.at[i], device)
        for i, (src, device, _, _) in enumerate(routes)
    ]
    for i in (4, 5, 6, 7, 2, 3, 0, 1):
        when(routes[i][2], rims[i].start)
    for i in range(8):
        when(routes[i][3], rims[i].wait_recv)
    has_low = jnp.where(lane < H, my_s, space - 1 - my_s) > 0
    upper, lower = unpack(rin[2], rin[3])
    upper = upper + jnp.where(my_k > 0, jnp.where(lane < H, rin[4], rin[5]), 0.0)
    lower = lower + jnp.where(my_k < groups - 1, jnp.where(lane < H, rin[6], rin[7]), 0.0)
    grad_ref[:H] = (
        gout[0, :H] + jnp.where(my_k > 0, rin[0], 0.0) + jnp.where(has_low, upper, 0.0)
    )
    grad_ref[H:] = (
        gout[0, H:N] + jnp.where(my_k < groups - 1, rin[1], 0.0) + jnp.where(has_low, lower, 0.0)
    )
    when(has_prev, halo[0].wait_send)
    when(has_next, halo[1].wait_send)
    for copy in [to_across, to_around] + first_group + second_group:
        copy.wait_send()
    for i in range(8):
        when(routes[i][2], rims[i].wait_send)


def body(space, groups, phase, target, kernels, weights):
    rows, cols = phase.shape
    count = kernels.shape[1]
    far = 8 if space % 16 == 0 else 1
    consts = [jnp.asarray(t) for t in tables()]
    vmem = pl.BlockSpec(memory_space=pltpu.VMEM)
    hbm = pl.BlockSpec(memory_space=pltpu.HBM)
    dma = pltpu.SemaphoreType.DMA
    return pl.pallas_call(
        functools.partial(kernel, space, groups, far),
        out_shape=[jax.ShapeDtypeStruct((N, cols), F32)] * 2,
        in_specs=[hbm] * 3 + [pl.BlockSpec(memory_space=pltpu.SMEM)] + [hbm] * 4,
        out_specs=[vmem, vmem],
        scratch_shapes=[
            pltpu.VMEM((rows, N), F32),
            pltpu.VMEM((N, N), jnp.int32),
            pltpu.VMEM((2, count, N + 1, N + 1), F32),
        ]
        + [pltpu.VMEM(t.shape, BF16) for t in consts]
        + [
            dma((6 + 2 * count,)),
            pltpu.VMEM((2 * N, N), F32),
            pltpu.VMEM((2, N, N), F32),
            pltpu.VMEM((2, N, N), F32),
            pltpu.VMEM((4, 2 * N, N), F32),
            pltpu.VMEM((2, 2, count * (N + 8) + 8, N), F32),
            pltpu.VMEM((groups, count, 4 * N, 2 * N), F32),
            pltpu.VMEM((4 * N, 2 * N), F32),
            pltpu.VMEM((groups, count * N, 2 * N), F32),
            pltpu.VMEM((4 * N, 2 * N), F32),
            pltpu.VMEM((2, 2 * N, N), F32),
            pltpu.VMEM((2, H, N), F32),
            pltpu.VMEM((8, H, N), F32),
            dma((2,)), dma((2,)),
            dma((6,)), dma((6,)),
            dma((8,)), dma((8,)),
        ],
        compiler_params=pltpu.CompilerParams(
            collective_id=0, has_side_effects=True, vmem_limit_bytes=int(53.8 * 2**20)
        ),
        cost_estimate=pl.CostEstimate(
            flops=14 * 10**9, bytes_accessed=4 * 10**6, transcendentals=0
        ),
        name="hopkins",
    )(phase, target, jnp.transpose(kernels, (0, 2, 1, 3)), weights, *consts)


def solution(mesh):
    placed = (P(None, "space"), P(None, "space"), P(None, "kern", None, None), P("kern"))
    return jax.shard_map(
        functools.partial(body, mesh.shape["space"], mesh.shape["kern"]),
        mesh=mesh,
        in_specs=placed,
        out_specs=(P("kern", "space"), P("kern", "space")),
        check_vma=False,
    )
```

```python
import functools

import jax
import jax.numpy as jnp
import ml_dtypes
import numpy as np
from jax import lax
from jax.experimental import pallas as pl
from jax.experimental.pallas import tpu as pltpu
from jax.sharding import PartitionSpec as P

STEEP = 2.5
LEVEL = 2.0
N = 128
H = 64
F32 = jnp.float32
BF16 = jnp.bfloat16
MESH = pl.DeviceIdType.MESH


def tables():
    x = np.arange(N)[:, None]
    k = np.arange(N)[None, :]
    parts = []
    for parity in (0, 1):
        angle = -2.0 * np.pi / (2 * N) * ((2 * k + parity) * x % (2 * N))
        c, s = np.cos(angle), np.sin(angle)
        parts.append(np.block([[c, s], [-s, c]]))
    full = np.concatenate(parts, axis=1)
    high = full.astype(ml_dtypes.bfloat16)
    low = (full - high.astype(np.float64)).astype(ml_dtypes.bfloat16)
    return high, low, np.ascontiguousarray(high.T), np.ascontiguousarray(low.T)


def cat(parts, axis):
    return jnp.concatenate(parts, axis=axis)


def split(x):
    high = x.astype(BF16)
    return high, (x - high.astype(F32)).astype(BF16)


def dot(a, b):
    return jnp.dot(a, b, preferred_element_type=F32)


def right(x, high, low):
    xh, xl = split(x)
    return dot(cat([xh, xl, xh], 1), cat([high, high, low], 0))


def left(high, low, x):
    xh, xl = split(x)
    return dot(cat([high, high, low], 1), cat([xh, xl, xh], 0))


def sincos(x):
    turn = jnp.floor(x * (2.0 / np.pi) + 0.5)
    r = x - turn * 1.5707855224609375
    r = r - turn * 1.0804273188e-05
    q = turn.astype(jnp.int32)
    z = r * r
    s = r + r * z * (-1.6666654611e-1 + z * (8.3321608736e-3 + z * -1.9515295891e-4))
    c = 1.0 - 0.5 * z + z * z * (
        4.166664568298827e-2 + z * (-1.388731625493765e-3 + z * 2.443315711809948e-5)
    )
    swap = (q & 1) != 0
    sin = jnp.where(swap, c, s)
    cos = jnp.where(swap, s, c)
    sin = jnp.where((q & 2) != 0, -sin, sin)
    cos = jnp.where(((q + 1) & 2) != 0, -cos, cos)
    return sin, cos


def flip(index, step):
    return index + step - 2 * step * lax.rem(index // step, 2)


def kernel(
    space, groups, far,
    phase_hbm, target_hbm, kern_hbm, weight_ref, fch_hbm, fcl_hbm, frh_hbm, frl_hbm,
    resist_ref, grad_ref,
    phase_ref, target_ref, kern_ref, fch, fcl, frh, frl, load_s,
    window, halo_out, halo_in, trig, raw, resp, spec, field, acc, gout, pout, cout, rin, cin,
    halo_s, halo_r, kern_s, kern_r, rim_s, rim_r,
):
    rows = phase_hbm.shape[0]
    count = kern_hbm.shape[2]
    my_k = lax.axis_index("kern")
    own = pl.multiple_of(my_k * N, N)
    pairs = [(phase_hbm, phase_ref)]
    pairs += [
        (kern_hbm.at[part, :, n], kern_ref.at[part, n]) for part in range(2) for n in range(count)
    ]
    pairs += [(fch_hbm, fch), (fcl_hbm, fcl), (frh_hbm, frh), (frl_hbm, frl)]
    pairs += [(target_hbm.at[pl.ds(own, N)], target_ref)]
    loads = [
        pltpu.make_async_copy(src, dst, load_s.at[i]) for i, (src, dst) in enumerate(pairs)
    ]
    for load in loads:
        load.start()
    tall = N + 8
    my_s = lax.axis_index("space")
    s_next = lax.rem(my_s + 1, space)
    s_prev = lax.rem(my_s + space - 1, space)
    k_next = lax.rem(my_k + 1, groups)
    k_prev = lax.rem(my_k + groups - 1, groups)
    sibling = (my_s, flip(my_k, 1))
    across = (my_s, flip(my_k, 2))
    around = (flip(my_s, far), flip(my_k, 2))

    mirror = (my_s, flip(flip(my_k, 1), 2))
    has_next, has_prev = my_s < space - 1, my_s > 0
    up, down = my_k < groups - 1, my_k > 0

    barrier = pltpu.get_barrier_semaphore()
    greeted = [
        (sibling, None), (across, None), (around, None), (mirror, up & down),
        ((s_next, my_k), has_next), ((s_prev, my_k), has_prev),
        ((s_next, k_next), has_next & up), ((s_next, k_prev), has_next & down),
        ((s_prev, k_next), has_prev & up), ((s_prev, k_prev), has_prev & down),
    ]

    def when(condition, action):
        if condition is None:
            action()
        else:
            pl.when(condition)(action)

    stage = pl.when(my_s >= 0)

    expected = 0
    for device, condition in greeted:
        when(
            condition,
            functools.partial(
                pl.semaphore_signal, barrier, inc=1, device_id=device, device_id_type=MESH
            ),
        )
        expected = expected + (1 if condition is None else jnp.where(condition, 1, 0))

    lane = lax.broadcasted_iota(jnp.int32, (8, N), 1)[:1]

    def pack(upper, lower):
        turned = pltpu.roll(lower, H, 1)
        return jnp.where(lane < H, upper, turned), jnp.where(lane < H, turned, upper)

    def unpack(low_side, high_side):
        upper = jnp.where(lane < H, low_side, high_side)
        return upper, pltpu.roll(jnp.where(lane < H, high_side, low_side), H, 1)

    def remote(src, dst, ssem, rsem, device):
        return pltpu.make_async_remote_copy(
            src_ref=src, dst_ref=dst, send_sem=ssem, recv_sem=rsem,
            device_id=device, device_id_type=MESH,
        )

    loads[0].wait()
    after = pl.multiple_of(jnp.minimum(own + N, rows - H), H)
    before = pl.multiple_of(jnp.maximum(own - H, 0), H)
    window[0:N] = phase_ref[pl.ds(own, N)]
    window[N : N + H] = phase_ref[pl.ds(after, H)]
    window[N + H :] = phase_ref[pl.ds(before, H)]
    halo_out[0], halo_out[1] = pack(window[:N], window[N:])
    halo = [
        remote(halo_out.at[0], halo_in.at[0], halo_s.at[0], halo_r.at[0], (s_prev, my_k)),
        remote(halo_out.at[1], halo_in.at[1], halo_s.at[1], halo_r.at[1], (s_next, my_k)),
    ]

    for load in loads[1 : 1 + 2 * count]:
        load.wait()
    gains = [
        jnp.sqrt(jnp.zeros((1, N), F32) + weight_ref[n]) * 2.0**-16 for n in range(count)
    ]
    for part in range(2):
        edges = jnp.zeros((8, N), F32)
        for n in range(count):
            gain = gains[n]
            raw[0, part, tall * n : tall * n + N] = (
                pltpu.roll(kern_ref[part, n, 0:N, 0:N], H, 1) * gain
            )
            last = jnp.broadcast_to(kern_ref[part, n, N : N + 1, 0:N], (8, N))
            raw[0, part, tall * n + N : tall * (n + 1)] = pltpu.roll(last, H, 1) * gain
            for g in range(N // 8 + 1):
                end = 8 * g + 8 if g < N // 8 else N + 1
                column = kern_ref[part, n, 8 * g : end, N : N + 1]
                edges = jnp.where(lane == count * g + n, column * gain, edges)
        raw[0, part, tall * count :] = edges

    pl.semaphore_wait(barrier, expected)
    when(has_prev, halo[0].start)
    when(has_next, halo[1].start)

    theirs = flip(my_k, 2)
    to_across = remote(raw.at[0, 0], raw.at[1, 0], kern_s.at[0], kern_r.at[0], across)
    to_around = remote(raw.at[0, 1], raw.at[1, 1], kern_s.at[1], kern_r.at[1], around)
    to_across.start()
    to_around.start()

    def shared(group, number, parity, index):
        half = resp.at[group, pl.ds(0, number), pl.ds(2 * N * parity, 2 * N)]
        return remote(half, half, kern_s.at[index], kern_r.at[index], sibling)

    def passed(part, index):
        span = pl.ds(tall * (count // 2), tall * (count - count // 2) + 8)
        return remote(
            raw.at[1, part, span], raw.at[2, part, span],
            kern_s.at[index], kern_r.at[index], sibling,
        )

    first_group = [shared(my_k, count, 0, 2), shared(my_k, count, 1, 3)]
    second_half = [shared(theirs, count // 2, 0, 4), shared(theirs, count // 2, 1, 5)]
    onward = [passed(0, 6), passed(1, 7)]

    sin, cos = sincos(window[...])
    row = lax.broadcasted_iota(jnp.int32, (2 * N, N), 0)
    missing = jnp.where((row >= N) & (row < N + H) & (my_k == groups - 1), 1, 0)
    missing = jnp.where((row >= N + H) & (my_k == 0), 1, missing)
    trig[0] = jnp.where(missing == 0, cos, 0.0)
    trig[1] = jnp.where(missing == 0, sin, 0.0)

    def respond_cols(slot, chosen):
        even, odd = [], []
        edges = [raw[slot, part, tall * count :] for part in range(2)]
        for n in chosen:
            pair = [[], []]
            for part in range(2):
                turned = raw[slot, part, tall * n : tall * (n + 1)]
                extra = cat(
                    [
                        jnp.where(
                            lane == H, edges[part][:, count * g + n : count * g + n + 1], 0.0
                        )
                        for g in range(N // 8 + 1)
                    ],
                    0,
                )
                pair[0].append(turned + extra)
                pair[1].append(jnp.where(lane < H, turned, -turned) + extra)
            even.append(cat(pair[0], 1))
            odd.append(cat(pair[1], 1))
        return (
            right(cat(even, 0), fch[:, : 2 * N], fcl[:, : 2 * N]),
            right(cat(odd, 0), fch[:, 2 * N :], fcl[:, 2 * N :]),
        )

    def respond(o, slot, chosen, copies):
        ge, go = respond_cols(slot, chosen)
        row = lax.broadcasted_iota(jnp.int32, (N, 2 * N), 0)
        even, odd = [], []
        for i in range(len(chosen)):
            pair = [[], []]
            at = slice(tall * i, tall * (i + 1))
            for c in (slice(0, N), slice(N, 2 * N)):
                g = cat([ge[at, c], go[at, c]], 1)
                extra = jnp.where(row == H, g[N : N + 1], 0.0)
                pair[0].append(cat([g[H:N], g[0:H]], 0) + extra)
                pair[1].append(cat([g[H:N], -g[0:H]], 0) + extra)
            even.append(cat(pair[0], 0))
            odd.append(cat(pair[1], 0))
        for p, x in enumerate((even, odd)):
            half = slice(2 * N * p, 2 * N * (p + 1))
            r = left(frh[half], frl[half], cat(x, 1))
            for i, n in enumerate(chosen):
                resp[o, n, half] = r[:, 2 * N * i : 2 * N * (i + 1)]
            if copies:
                copies[p].start()

    def members(owners):
        return [(o, n) for o in owners for n in range(count)]

    def field_rows(owners):
        xs = []
        for o, n in members(owners):
            parts = []
            for p in range(2):
                low = slice(2 * N * p, 2 * N * p + N)
                high = slice(2 * N * p + N, 2 * N * (p + 1))
                rr, ri = resp[o, n, low], resp[o, n, high]
                sr, si = spec[low], spec[high]
                parts += [rr * sr - ri * si, rr * si + ri * sr]
            xs.append(cat(parts, 0))
        return left(fch[...], fcl[...], cat(xs, 1))

    def fields(owners):
        z = field_rows(owners)
        zs = []
        for n in range(len(owners) * count):
            q = z[:, 2 * N * n : 2 * N * (n + 1)]
            zs.append(cat([q[:N, :N], q[N:, :N], q[:N, N:], q[N:, N:]], 1))
        f = right(cat(zs, 0), frh[...], frl[...])
        for i, o in enumerate(owners):
            field[o] = f[N * count * i : N * count * (i + 1)]
        q = f * f
        total = None
        for n in range(len(owners) * count):
            g = q[N * n : N * (n + 1)]
            term = g[:, :N] + g[:, N:]
            total = term if total is None else total + term
        return total

    for load in loads[1 + 2 * count :]:
        load.wait()
    respond(my_k, 0, range(count), first_group)

    when(has_next, halo[0].wait_recv)
    when(has_prev, halo[1].wait_recv)
    upper, lower = unpack(halo_in[0], halo_in[1])
    sin, cos = sincos(cat([upper, lower], 0))
    inside = jnp.where(lane < H, space - 1 - my_s, my_s) > 0
    cos = jnp.where(inside & (missing == 0), cos, 0.0)
    sin = jnp.where(inside & (missing == 0), sin, 0.0)
    trig[2] = cos
    trig[3] = sin
    se = right(
        cat([trig[0] + cos, trig[1] + sin], 1), fch[:, : 2 * N], fcl[:, : 2 * N]
    )
    so = right(
        cat([trig[0] - cos, trig[1] - sin], 1), fch[:, 2 * N :], fcl[:, 2 * N :]
    )
    even, odd = [], []
    for c in (slice(0, N), slice(N, 2 * N)):
        g = cat([se[:, c], so[:, c]], 1)
        even.append(g[:N] + g[N:])
        odd.append(g[:N] - g[N:])
    spec[: 2 * N] = left(frh[: 2 * N], frl[: 2 * N], cat(even, 0))
    spec[2 * N :] = left(frh[2 * N :], frl[2 * N :], cat(odd, 0))

    kin, theirs_kin = flip(my_k, 1), flip(theirs, 1)
    for copy in first_group:
        copy.wait_recv()
    intensity = fields((my_k, kin))

    @stage
    def _():
        to_across.wait_recv()
        to_around.wait_recv()
        for copy in onward:
            copy.start()
        respond(theirs, 1, range(count), second_half)

    intensity = intensity + fields((theirs,))

    @stage
    def _():
        for copy in onward:
            copy.wait_recv()
        respond(theirs_kin, 2, range(count // 2, count), None)
        for copy in second_half:
            copy.wait_recv()

    intensity = intensity + fields((theirs_kin,))

    resist = 1.0 / (1.0 + jnp.exp(-STEEP * (intensity - LEVEL)))
    resist_ref[...] = resist
    want = target_ref[...].astype(F32)
    factor = 4.0 * STEEP * (resist - want) * resist * (1.0 - resist)

    def pulls(owners):
        xs = []
        for o, n in members(owners):
            f = field[o, N * n : N * (n + 1)]
            xs.append(cat([factor * f[:, :N], factor * f[:, N:]], 1))
        y = right(cat(xs, 0), fch[...], fcl[...])
        xs = []
        for i in range(len(owners) * count):
            q = y[N * i : N * (i + 1)]
            re = cat([q[:, :N], q[:, 2 * N : 3 * N]], 1)
            im = cat([q[:, N : 2 * N], q[:, 3 * N :]], 1)
            xs.append(cat([re, im], 0))
        v = left(frh[...], frl[...], cat(xs, 1))
        for p in range(2):
            low = slice(2 * N * p, 2 * N * p + N)
            high = slice(2 * N * p + N, 2 * N * (p + 1))
            re, im = acc[low], acc[high]
            for i, (o, n) in enumerate(members(owners)):
                rr, ri = resp[o, n, low], resp[o, n, high]
                vr = v[low, 2 * N * i : 2 * N * (i + 1)]
                vi = v[high, 2 * N * i : 2 * N * (i + 1)]
                re = re + (rr * vr + ri * vi)
                im = im + (rr * vi - ri * vr)
            acc[low] = re
            acc[high] = im

    acc[...] = jnp.zeros((4 * N, 2 * N), F32)

    def pull_step(j, carry):
        low = jnp.where(j == 0, my_k, theirs)
        pulls((low, flip(low, 1)))
        return carry

    lax.fori_loop(0, 2, pull_step, 0)

    e = left(fch[:, : 2 * N], fcl[:, : 2 * N], acc[: 2 * N])
    o = left(fch[:, 2 * N :], fcl[:, 2 * N :], acc[2 * N :])
    u, v = e + o, e - o
    br = cat([u[:N], v[:N]], 0)
    bi = cat([u[N:], v[N:]], 0)
    e = right(cat([br[:, :N], bi[:, :N]], 1), frh[: 2 * N], frl[: 2 * N])
    o = right(cat([br[:, N:], bi[:, N:]], 1), frh[2 * N :], frl[2 * N :])
    u, v = e + o, e - o
    gout[...] = u[:, N:] * trig[0] - u[:, :N] * trig[1]
    side = v[:, N:] * trig[2] - v[:, :N] * trig[3]
    pout[0], pout[1] = pack(side[:H], side[H:N])
    quarter = H // 2
    cout[0], cout[1] = pack(side[N : N + quarter], side[N + quarter : N + H])
    cout[2], cout[3] = pack(side[N + H : N + H + quarter], side[N + H + quarter :])
    low_rows, high_rows = pl.ds(N, H), pl.ds(N + H, H)
    routes = [
        (gout.at[low_rows], (my_s, k_next), up, down),
        (gout.at[high_rows], (my_s, k_prev), down, up),
        (pout.at[0], (s_next, my_k), has_next, has_prev),
        (pout.at[1], (s_prev, my_k), has_prev, has_next),
        (cout.at[0], (s_next, k_next), has_next & up, has_prev & down),
        (cout.at[1], (s_prev, k_next), has_prev & up, has_next & down),
        (cout.at[2], (s_next, k_prev), has_next & down, has_prev & up),
        (cout.at[3], (s_prev, k_prev), has_prev & down, has_next & up),
    ]
    rims = [
        remote(src, rin.at[i] if i < 4 else cin.at[i - 4], rim_s.at[i], rim_r.at[i], device)
        for i, (src, device, _, _) in enumerate(routes)
    ]
    for i in (2, 3, 4, 5, 6, 7, 0, 1):
        when(routes[i][2], rims[i].start)
    for i in range(8):
        when(routes[i][3], rims[i].wait_recv)
    has_low = jnp.where(lane < H, my_s, space - 1 - my_s) > 0
    upper, lower = unpack(rin[2], rin[3])
    upper = upper + jnp.where(down, cat(unpack(cin[0], cin[1]), 0), 0.0)
    lower = lower + jnp.where(up, cat(unpack(cin[2], cin[3]), 0), 0.0)
    grad_ref[:H] = (
        gout[:H] + jnp.where(my_k > 0, rin[0], 0.0) + jnp.where(has_low, upper, 0.0)
    )
    grad_ref[H:] = (
        gout[H:N] + jnp.where(my_k < groups - 1, rin[1], 0.0) + jnp.where(has_low, lower, 0.0)
    )
    when(has_prev, halo[0].wait_send)
    when(has_next, halo[1].wait_send)
    for copy in [to_across, to_around] + first_group + second_half + onward:
        copy.wait_send()
    for i in range(8):
        when(routes[i][2], rims[i].wait_send)


def body(space, groups, phase, target, kernels, weights):
    rows, cols = phase.shape
    count = kernels.shape[1]
    far = 8 if space % 16 == 0 else 1
    consts = [jnp.asarray(t) for t in tables()]
    vmem = pl.BlockSpec(memory_space=pltpu.VMEM)
    hbm = pl.BlockSpec(memory_space=pltpu.HBM)
    dma = pltpu.SemaphoreType.DMA
    return pl.pallas_call(
        functools.partial(kernel, space, groups, far),
        out_shape=[jax.ShapeDtypeStruct((N, cols), F32)] * 2,
        in_specs=[hbm] * 3 + [pl.BlockSpec(memory_space=pltpu.SMEM)] + [hbm] * 4,
        out_specs=[vmem, vmem],
        scratch_shapes=[
            pltpu.VMEM((rows, N), F32),
            pltpu.VMEM((N, N), jnp.int32),
            pltpu.VMEM((2, count, N + 1, N + 1), F32),
        ]
        + [pltpu.VMEM(t.shape, BF16) for t in consts]
        + [
            dma((6 + 2 * count,)),
            pltpu.VMEM((2 * N, N), F32),
            pltpu.VMEM((2, N, N), F32),
            pltpu.VMEM((2, N, N), F32),
            pltpu.VMEM((4, 2 * N, N), F32),
            pltpu.VMEM((3, 2, count * (N + 8) + 8, N), F32),
            pltpu.VMEM((groups, count, 4 * N, 2 * N), F32),
            pltpu.VMEM((4 * N, 2 * N), F32),
            pltpu.VMEM((groups, count * N, 2 * N), F32),
            pltpu.VMEM((4 * N, 2 * N), F32),
            pltpu.VMEM((2 * N, N), F32),
            pltpu.VMEM((2, H, N), F32),
            pltpu.VMEM((4, H // 2, N), F32),
            pltpu.VMEM((4, H, N), F32),
            pltpu.VMEM((4, H // 2, N), F32),
            dma((2,)), dma((2,)),
            dma((8,)), dma((8,)),
            dma((8,)), dma((8,)),
        ],
        compiler_params=pltpu.CompilerParams(
            collective_id=0, has_side_effects=True, vmem_limit_bytes=int(53.8 * 2**20)
        ),
        cost_estimate=pl.CostEstimate(
            flops=14 * 10**9, bytes_accessed=4 * 10**6, transcendentals=0
        ),
        name="hopkins",
    )(phase, target, jnp.transpose(kernels, (0, 2, 1, 3)), weights, *consts)


def solution(mesh):
    placed = (P(None, "space"), P(None, "space"), P(None, "kern", None, None), P("kern"))
    return jax.shard_map(
        functools.partial(body, mesh.shape["space"], mesh.shape["kern"]),
        mesh=mesh,
        in_specs=placed,
        out_specs=(P("kern", "space"), P("kern", "space")),
        check_vma=False,
    )
```

```python
import functools

import jax
import jax.numpy as jnp
import ml_dtypes
import numpy as np
from jax import lax
from jax.experimental import pallas as pl
from jax.experimental.pallas import tpu as pltpu
from jax.sharding import PartitionSpec as P

STEEP = 2.5
LEVEL = 2.0
N = 128
H = 64
F32 = jnp.float32
BF16 = jnp.bfloat16
MESH = pl.DeviceIdType.MESH


def tables():
    x = np.arange(N)[:, None]
    k = np.arange(N)[None, :]
    parts = []
    for parity in (0, 1):
        angle = -2.0 * np.pi / (2 * N) * ((2 * k + parity) * x % (2 * N))
        c, s = np.cos(angle), np.sin(angle)
        parts.append(np.block([[c, s], [-s, c]]))
    full = np.concatenate(parts, axis=1)
    high = full.astype(ml_dtypes.bfloat16)
    low = (full - high.astype(np.float64)).astype(ml_dtypes.bfloat16)
    return high, low, np.ascontiguousarray(high.T), np.ascontiguousarray(low.T)


def cat(parts, axis):
    return jnp.concatenate(parts, axis=axis)


def split(x):
    high = x.astype(BF16)
    return high, (x - high.astype(F32)).astype(BF16)


def dot(a, b):
    return jnp.dot(a, b, preferred_element_type=F32)


def right(x, high, low):
    xh, xl = split(x)
    return dot(cat([xh, xl, xh], 1), cat([high, high, low], 0))


def left(high, low, x):
    xh, xl = split(x)
    return dot(cat([high, high, low], 1), cat([xh, xl, xh], 0))


def sincos(x):
    turn = jnp.floor(x * (2.0 / np.pi) + 0.5)
    r = x - turn * 1.5707855224609375
    r = r - turn * 1.0804273188e-05
    q = turn.astype(jnp.int32)
    z = r * r
    s = r + r * z * (-1.6666654611e-1 + z * (8.3321608736e-3 + z * -1.9515295891e-4))
    c = 1.0 - 0.5 * z + z * z * (
        4.166664568298827e-2 + z * (-1.388731625493765e-3 + z * 2.443315711809948e-5)
    )
    swap = (q & 1) != 0
    sin = jnp.where(swap, c, s)
    cos = jnp.where(swap, s, c)
    sin = jnp.where((q & 2) != 0, -sin, sin)
    cos = jnp.where(((q + 1) & 2) != 0, -cos, cos)
    return sin, cos


def flip(index, step):
    return index + step - 2 * step * lax.rem(index // step, 2)


def kernel(
    space, groups, far,
    phase_hbm, target_hbm, kern_hbm, weight_ref, fch_hbm, fcl_hbm, frh_hbm, frl_hbm,
    out_ref,
    phase_ref, target_ref, kern_ref, fch, fcl, frh, frl, load_s,
    window, halo_out, halo_in, trig, raw, resp, spec, field, acc, gout, pout, cout, rin, cin,
    halo_s, halo_r, kern_s, kern_r, rim_s, rim_r,
):
    rows = phase_hbm.shape[0]
    count = kern_hbm.shape[2]
    my_k = lax.axis_index("kern")
    own = pl.multiple_of(my_k * N, N)
    pairs = [(phase_hbm, phase_ref)]
    pairs += [
        (kern_hbm.at[part, :, n], kern_ref.at[part, n]) for part in range(2) for n in range(count)
    ]
    pairs += [(fch_hbm, fch), (fcl_hbm, fcl), (frh_hbm, frh), (frl_hbm, frl)]
    pairs += [(target_hbm.at[pl.ds(own, N)], target_ref)]
    loads = [
        pltpu.make_async_copy(src, dst, load_s.at[i]) for i, (src, dst) in enumerate(pairs)
    ]
    loads[0].start()
    tall = N + 8
    my_s = lax.axis_index("space")
    s_next = lax.rem(my_s + 1, space)
    s_prev = lax.rem(my_s + space - 1, space)
    k_next = lax.rem(my_k + 1, groups)
    k_prev = lax.rem(my_k + groups - 1, groups)
    sibling = (my_s, flip(my_k, 1))
    across = (my_s, flip(my_k, 2))
    around = (flip(my_s, far), flip(my_k, 2))

    mirror = (my_s, flip(flip(my_k, 1), 2))
    has_next, has_prev = my_s < space - 1, my_s > 0
    up, down = my_k < groups - 1, my_k > 0

    barrier = pltpu.get_barrier_semaphore()
    greeted = [
        ((s_next, k_next), has_next & up), ((s_next, k_prev), has_next & down),
        ((s_prev, k_next), has_prev & up), ((s_prev, k_prev), has_prev & down),
        ((s_next, my_k), has_next), ((s_prev, my_k), has_prev),
        (around, None), (across, None), (mirror, up & down), (sibling, None),
    ]

    def when(condition, action):
        if condition is None:
            action()
        else:
            pl.when(condition)(action)

    stage = pl.when(my_s >= 0)

    expected = 0
    for device, condition in greeted:
        when(
            condition,
            functools.partial(
                pl.semaphore_signal, barrier, inc=1, device_id=device, device_id_type=MESH
            ),
        )
        expected = expected + (1 if condition is None else jnp.where(condition, 1, 0))

    for load in loads[1:]:
        load.start()

    lane = lax.broadcasted_iota(jnp.int32, (8, N), 1)[:1]

    def pack(upper, lower):
        turned = pltpu.roll(lower, H, 1)
        return jnp.where(lane < H, upper, turned), jnp.where(lane < H, turned, upper)

    def unpack(low_side, high_side):
        upper = jnp.where(lane < H, low_side, high_side)
        return upper, pltpu.roll(jnp.where(lane < H, high_side, low_side), H, 1)

    def remote(src, dst, ssem, rsem, device):
        return pltpu.make_async_remote_copy(
            src_ref=src, dst_ref=dst, send_sem=ssem, recv_sem=rsem,
            device_id=device, device_id_type=MESH,
        )

    loads[0].wait()
    after = pl.multiple_of(jnp.minimum(own + N, rows - H), H)
    before = pl.multiple_of(jnp.maximum(own - H, 0), H)
    window[0:N] = phase_ref[pl.ds(own, N)]
    window[N : N + H] = phase_ref[pl.ds(after, H)]
    window[N + H :] = phase_ref[pl.ds(before, H)]
    halo_out[0], halo_out[1] = pack(window[:N], window[N:])
    halo = [
        remote(halo_out.at[0], halo_in.at[0], halo_s.at[0], halo_r.at[0], (s_prev, my_k)),
        remote(halo_out.at[1], halo_in.at[1], halo_s.at[1], halo_r.at[1], (s_next, my_k)),
    ]

    for load in loads[1 : 1 + 2 * count]:
        load.wait()
    gains = [
        jnp.sqrt(jnp.zeros((1, N), F32) + weight_ref[n]) * 2.0**-16 for n in range(count)
    ]
    for part in range(2):
        edges = jnp.zeros((8, N), F32)
        for n in range(count):
            gain = gains[n]
            raw[0, part, tall * n : tall * n + N] = (
                pltpu.roll(kern_ref[part, n, 0:N, 0:N], H, 1) * gain
            )
            last = jnp.broadcast_to(kern_ref[part, n, N : N + 1, 0:N], (8, N))
            raw[0, part, tall * n + N : tall * (n + 1)] = pltpu.roll(last, H, 1) * gain
            for g in range(N // 8 + 1):
                end = 8 * g + 8 if g < N // 8 else N + 1
                column = kern_ref[part, n, 8 * g : end, N : N + 1]
                edges = jnp.where(lane == count * g + n, column * gain, edges)
        raw[0, part, tall * count :] = edges

    pl.semaphore_wait(barrier, expected)
    when(has_prev, halo[0].start)
    when(has_next, halo[1].start)

    theirs = flip(my_k, 2)
    to_across = remote(raw.at[0, 0], raw.at[1, 0], kern_s.at[0], kern_r.at[0], across)
    to_around = remote(raw.at[0, 1], raw.at[1, 1], kern_s.at[1], kern_r.at[1], around)
    to_across.start()
    to_around.start()

    def shared(group, number, parity, index):
        half = resp.at[group, pl.ds(0, number), pl.ds(2 * N * parity, 2 * N)]
        return remote(half, half, kern_s.at[index], kern_r.at[index], sibling)

    def passed(part, index):
        span = pl.ds(tall * (count // 2), tall * (count - count // 2) + 8)
        return remote(
            raw.at[1, part, span], raw.at[2, part, span],
            kern_s.at[index], kern_r.at[index], sibling,
        )

    first_group = [shared(my_k, count, 0, 2), shared(my_k, count, 1, 3)]
    second_half = [shared(theirs, count // 2, 0, 4), shared(theirs, count // 2, 1, 5)]
    onward = [passed(0, 6), passed(1, 7)]

    sin, cos = sincos(window[...])
    row = lax.broadcasted_iota(jnp.int32, (2 * N, N), 0)
    missing = jnp.where((row >= N) & (row < N + H) & (my_k == groups - 1), 1, 0)
    missing = jnp.where((row >= N + H) & (my_k == 0), 1, missing)
    trig[0] = jnp.where(missing == 0, cos, 0.0)
    trig[1] = jnp.where(missing == 0, sin, 0.0)

    def respond_cols(slot, chosen):
        even, odd = [], []
        edges = [raw[slot, part, tall * count :] for part in range(2)]
        for n in chosen:
            pair = [[], []]
            for part in range(2):
                turned = raw[slot, part, tall * n : tall * (n + 1)]
                extra = cat(
                    [
                        jnp.where(
                            lane == H, edges[part][:, count * g + n : count * g + n + 1], 0.0
                        )
                        for g in range(N // 8 + 1)
                    ],
                    0,
                )
                pair[0].append(turned + extra)
                pair[1].append(jnp.where(lane < H, turned, -turned) + extra)
            even.append(cat(pair[0], 1))
            odd.append(cat(pair[1], 1))
        return (
            right(cat(even, 0), fch[:, : 2 * N], fcl[:, : 2 * N]),
            right(cat(odd, 0), fch[:, 2 * N :], fcl[:, 2 * N :]),
        )

    def respond(o, slot, chosen, copies):
        ge, go = respond_cols(slot, chosen)
        row = lax.broadcasted_iota(jnp.int32, (N, 2 * N), 0)
        even, odd = [], []
        for i in range(len(chosen)):
            pair = [[], []]
            at = slice(tall * i, tall * (i + 1))
            for c in (slice(0, N), slice(N, 2 * N)):
                g = cat([ge[at, c], go[at, c]], 1)
                extra = jnp.where(row == H, g[N : N + 1], 0.0)
                pair[0].append(cat([g[H:N], g[0:H]], 0) + extra)
                pair[1].append(cat([g[H:N], -g[0:H]], 0) + extra)
            even.append(cat(pair[0], 0))
            odd.append(cat(pair[1], 0))
        for p, x in enumerate((even, odd)):
            half = slice(2 * N * p, 2 * N * (p + 1))
            r = left(frh[half], frl[half], cat(x, 1))
            for i, n in enumerate(chosen):
                resp[o, n, half] = r[:, 2 * N * i : 2 * N * (i + 1)]
            if copies:
                copies[p].start()

    def members(owners):
        return [(o, n) for o in owners for n in range(count)]

    def field_rows(owners):
        xs = []
        for o, n in members(owners):
            parts = []
            for p in range(2):
                low = slice(2 * N * p, 2 * N * p + N)
                high = slice(2 * N * p + N, 2 * N * (p + 1))
                rr, ri = resp[o, n, low], resp[o, n, high]
                sr, si = spec[low], spec[high]
                parts += [rr * sr - ri * si, rr * si + ri * sr]
            xs.append(cat(parts, 0))
        return left(fch[...], fcl[...], cat(xs, 1))

    def fields(owners):
        z = field_rows(owners)
        zs = []
        for n in range(len(owners) * count):
            q = z[:, 2 * N * n : 2 * N * (n + 1)]
            zs.append(cat([q[:N, :N], q[N:, :N], q[:N, N:], q[N:, N:]], 1))
        f = right(cat(zs, 0), frh[...], frl[...])
        for i, o in enumerate(owners):
            field[o] = f[N * count * i : N * count * (i + 1)]
        q = f * f
        total = None
        for n in range(len(owners) * count):
            g = q[N * n : N * (n + 1)]
            term = g[:, :N] + g[:, N:]
            total = term if total is None else total + term
        return total

    for load in loads[1 + 2 * count :]:
        load.wait()
    respond(my_k, 0, range(count), first_group)

    when(has_next, halo[0].wait_recv)
    when(has_prev, halo[1].wait_recv)
    upper, lower = unpack(halo_in[0], halo_in[1])
    sin, cos = sincos(cat([upper, lower], 0))
    inside = jnp.where(lane < H, space - 1 - my_s, my_s) > 0
    cos = jnp.where(inside & (missing == 0), cos, 0.0)
    sin = jnp.where(inside & (missing == 0), sin, 0.0)
    trig[2] = cos
    trig[3] = sin
    se = right(
        cat([trig[0] + cos, trig[1] + sin], 1), fch[:, : 2 * N], fcl[:, : 2 * N]
    )
    so = right(
        cat([trig[0] - cos, trig[1] - sin], 1), fch[:, 2 * N :], fcl[:, 2 * N :]
    )
    even, odd = [], []
    for c in (slice(0, N), slice(N, 2 * N)):
        g = cat([se[:, c], so[:, c]], 1)
        even.append(g[:N] + g[N:])
        odd.append(g[:N] - g[N:])
    spec[: 2 * N] = left(frh[: 2 * N], frl[: 2 * N], cat(even, 0))
    spec[2 * N :] = left(frh[2 * N :], frl[2 * N :], cat(odd, 0))

    kin, theirs_kin = flip(my_k, 1), flip(theirs, 1)
    for copy in first_group:
        copy.wait_recv()
    intensity = fields((my_k, kin))

    @stage
    def _():
        to_across.wait_recv()
        to_around.wait_recv()
        for copy in onward:
            copy.start()
        respond(theirs, 1, range(count), second_half)

    intensity = intensity + fields((theirs,))

    @stage
    def _():
        for copy in onward:
            copy.wait_recv()
        respond(theirs_kin, 2, range(count // 2, count), None)
        for copy in second_half:
            copy.wait_recv()

    intensity = intensity + fields((theirs_kin,))

    resist = 1.0 / (1.0 + jnp.exp(-STEEP * (intensity - LEVEL)))
    out_ref[0] = resist
    want = target_ref[...].astype(F32)
    factor = 4.0 * STEEP * (resist - want) * resist * (1.0 - resist)

    def pulls(owners):
        xs = []
        for o, n in members(owners):
            f = field[o, N * n : N * (n + 1)]
            xs.append(cat([factor * f[:, :N], factor * f[:, N:]], 1))
        y = right(cat(xs, 0), fch[...], fcl[...])
        xs = []
        for i in range(len(owners) * count):
            q = y[N * i : N * (i + 1)]
            re = cat([q[:, :N], q[:, 2 * N : 3 * N]], 1)
            im = cat([q[:, N : 2 * N], q[:, 3 * N :]], 1)
            xs.append(cat([re, im], 0))
        v = left(frh[...], frl[...], cat(xs, 1))
        for p in range(2):
            low = slice(2 * N * p, 2 * N * p + N)
            high = slice(2 * N * p + N, 2 * N * (p + 1))
            re, im = acc[low], acc[high]
            for i, (o, n) in enumerate(members(owners)):
                rr, ri = resp[o, n, low], resp[o, n, high]
                vr = v[low, 2 * N * i : 2 * N * (i + 1)]
                vi = v[high, 2 * N * i : 2 * N * (i + 1)]
                re = re + (rr * vr + ri * vi)
                im = im + (rr * vi - ri * vr)
            acc[low] = re
            acc[high] = im

    acc[...] = jnp.zeros((4 * N, 2 * N), F32)

    def pull_step(j, carry):
        low = jnp.where(j == 0, my_k, theirs)
        pulls((low, flip(low, 1)))
        return carry

    lax.fori_loop(0, 2, pull_step, 0)

    e = left(fch[:, : 2 * N], fcl[:, : 2 * N], acc[: 2 * N])
    o = left(fch[:, 2 * N :], fcl[:, 2 * N :], acc[2 * N :])
    u, v = e + o, e - o
    br = cat([u[:N], v[:N]], 0)
    bi = cat([u[N:], v[N:]], 0)
    e = right(cat([br[:, :N], bi[:, :N]], 1), frh[: 2 * N], frl[: 2 * N])
    o = right(cat([br[:, N:], bi[:, N:]], 1), frh[2 * N :], frl[2 * N :])
    u, v = e + o, e - o
    gout[...] = u[:, N:] * trig[0] - u[:, :N] * trig[1]
    side = v[:, N:] * trig[2] - v[:, :N] * trig[3]
    pout[0], pout[1] = pack(side[:H], side[H:N])
    quarter = H // 2
    cout[0], cout[1] = pack(side[N : N + quarter], side[N + quarter : N + H])
    cout[2], cout[3] = pack(side[N + H : N + H + quarter], side[N + H + quarter :])
    low_rows, high_rows = pl.ds(N, H), pl.ds(N + H, H)
    routes = [
        (gout.at[low_rows], (my_s, k_next), up, down),
        (gout.at[high_rows], (my_s, k_prev), down, up),
        (pout.at[0], (s_next, my_k), has_next, has_prev),
        (pout.at[1], (s_prev, my_k), has_prev, has_next),
        (cout.at[0], (s_next, k_next), has_next & up, has_prev & down),
        (cout.at[1], (s_prev, k_next), has_prev & up, has_next & down),
        (cout.at[2], (s_next, k_prev), has_next & down, has_prev & up),
        (cout.at[3], (s_prev, k_prev), has_prev & down, has_next & up),
    ]
    rims = [
        remote(src, rin.at[i] if i < 4 else cin.at[i - 4], rim_s.at[i], rim_r.at[i], device)
        for i, (src, device, _, _) in enumerate(routes)
    ]
    for i in (2, 3, 4, 5, 6, 7, 0, 1):
        when(routes[i][2], rims[i].start)
    for i in range(8):
        when(routes[i][3], rims[i].wait_recv)
    has_low = jnp.where(lane < H, my_s, space - 1 - my_s) > 0
    upper, lower = unpack(rin[2], rin[3])
    upper = upper + jnp.where(down, cat(unpack(cin[0], cin[1]), 0), 0.0)
    lower = lower + jnp.where(up, cat(unpack(cin[2], cin[3]), 0), 0.0)
    out_ref[1, :H] = (
        gout[:H] + jnp.where(my_k > 0, rin[0], 0.0) + jnp.where(has_low, upper, 0.0)
    )
    out_ref[1, H:] = (
        gout[H:N] + jnp.where(my_k < groups - 1, rin[1], 0.0) + jnp.where(has_low, lower, 0.0)
    )
    when(has_prev, halo[0].wait_send)
    when(has_next, halo[1].wait_send)
    for copy in [to_across, to_around] + first_group + second_half + onward:
        copy.wait_send()
    for i in range(8):
        when(routes[i][2], rims[i].wait_send)


def body(space, groups, phase, target, kernels, weights):
    rows, cols = phase.shape
    count = kernels.shape[1]
    far = 8 if space % 16 == 0 else 1
    consts = [jnp.asarray(t) for t in tables()]
    vmem = pl.BlockSpec(memory_space=pltpu.VMEM)
    hbm = pl.BlockSpec(memory_space=pltpu.HBM)
    dma = pltpu.SemaphoreType.DMA
    out = pl.pallas_call(
        functools.partial(kernel, space, groups, far),
        out_shape=jax.ShapeDtypeStruct((2, N, cols), F32),
        in_specs=[hbm] * 3 + [pl.BlockSpec(memory_space=pltpu.SMEM)] + [hbm] * 4,
        out_specs=vmem,
        scratch_shapes=[
            pltpu.VMEM((rows, N), F32),
            pltpu.VMEM((N, N), jnp.int32),
            pltpu.VMEM((2, count, N + 1, N + 1), F32),
        ]
        + [pltpu.VMEM(t.shape, BF16) for t in consts]
        + [
            dma((6 + 2 * count,)),
            pltpu.VMEM((2 * N, N), F32),
            pltpu.VMEM((2, N, N), F32),
            pltpu.VMEM((2, N, N), F32),
            pltpu.VMEM((4, 2 * N, N), F32),
            pltpu.VMEM((3, 2, count * (N + 8) + 8, N), F32),
            pltpu.VMEM((groups, count, 4 * N, 2 * N), F32),
            pltpu.VMEM((4 * N, 2 * N), F32),
            pltpu.VMEM((groups, count * N, 2 * N), F32),
            pltpu.VMEM((4 * N, 2 * N), F32),
            pltpu.VMEM((2 * N, N), F32),
            pltpu.VMEM((2, H, N), F32),
            pltpu.VMEM((4, H // 2, N), F32),
            pltpu.VMEM((4, H, N), F32),
            pltpu.VMEM((4, H // 2, N), F32),
            dma((2,)), dma((2,)),
            dma((8,)), dma((8,)),
            dma((8,)), dma((8,)),
        ],
        compiler_params=pltpu.CompilerParams(
            collective_id=0, has_side_effects=True, vmem_limit_bytes=int(53.8 * 2**20)
        ),
        cost_estimate=pl.CostEstimate(
            flops=14 * 10**9, bytes_accessed=4 * 10**6, transcendentals=0
        ),
        name="hopkins",
    )(phase, target, jnp.transpose(kernels, (0, 2, 1, 3)), weights, *consts)
    return (out[0], out[1])


def solution(mesh):
    placed = (P(None, "space"), P(None, "space"), P(None, "kern", None, None), P("kern"))
    return jax.shard_map(
        functools.partial(body, mesh.shape["space"], mesh.shape["kern"]),
        mesh=mesh,
        in_specs=placed,
        out_specs=(P("kern", "space"), P("kern", "space")),
        check_vma=False,
    )
```

```python
import functools

import jax
import jax.numpy as jnp
import ml_dtypes
import numpy as np
from jax import lax
from jax.experimental import pallas as pl
from jax.experimental.pallas import tpu as pltpu
from jax.sharding import PartitionSpec as P

STEEP = 2.5
LEVEL = 2.0
N = 128
H = 64
F32 = jnp.float32
BF16 = jnp.bfloat16
MESH = pl.DeviceIdType.MESH


def tables():
    x = np.arange(N)[:, None]
    k = np.arange(N)[None, :]
    parts = []
    for parity in (0, 1):
        angle = -2.0 * np.pi / (2 * N) * ((2 * k + parity) * x % (2 * N))
        c, s = np.cos(angle), np.sin(angle)
        parts.append(np.block([[c, s], [-s, c]]))
    full = np.concatenate(parts, axis=1)
    high = full.astype(ml_dtypes.bfloat16)
    low = (full - high.astype(np.float64)).astype(ml_dtypes.bfloat16)
    return high, low, np.ascontiguousarray(high.T), np.ascontiguousarray(low.T)


def cat(parts, axis):
    return jnp.concatenate(parts, axis=axis)


def split(x):
    high = x.astype(BF16)
    return high, (x - high.astype(F32)).astype(BF16)


def dot(a, b):
    return jnp.dot(a, b, preferred_element_type=F32)


def right(x, high, low):
    xh, xl = split(x)
    return dot(cat([xh, xl, xh], 1), cat([high, high, low], 0))


def left(high, low, x):
    xh, xl = split(x)
    return dot(cat([high, high, low], 1), cat([xh, xl, xh], 0))


def sincos(x):
    turn = jnp.floor(x * (2.0 / np.pi) + 0.5)
    r = x - turn * 1.5707855224609375
    r = r - turn * 1.0804273188e-05
    q = turn.astype(jnp.int32)
    z = r * r
    s = r + r * z * (-1.6666654611e-1 + z * (8.3321608736e-3 + z * -1.9515295891e-4))
    c = 1.0 - 0.5 * z + z * z * (
        4.166664568298827e-2 + z * (-1.388731625493765e-3 + z * 2.443315711809948e-5)
    )
    swap = (q & 1) != 0
    sin = jnp.where(swap, c, s)
    cos = jnp.where(swap, s, c)
    sin = jnp.where((q & 2) != 0, -sin, sin)
    cos = jnp.where(((q + 1) & 2) != 0, -cos, cos)
    return sin, cos


def flip(index, step):
    return index + step - 2 * step * lax.rem(index // step, 2)


def kernel(
    space, groups, far,
    phase_hbm, target_hbm, kern_hbm, weight_ref, fch_hbm, fcl_hbm, frh_hbm, frl_hbm,
    out_ref,
    phase_ref, target_ref, kern_ref, fch, fcl, frh, frl, load_s,
    window, halo_out, halo_in, trig, raw, resp, spec, field, acc, gout, pout, cout, rin, cin,
    halo_s, halo_r, kern_s, kern_r, rim_s, rim_r,
):
    rows = phase_hbm.shape[0]
    count = kern_hbm.shape[2]
    my_k = lax.axis_index("kern")
    own = pl.multiple_of(my_k * N, N)
    pairs = [(phase_hbm, phase_ref)]
    pairs += [
        (kern_hbm.at[part, :, n], kern_ref.at[part, n]) for part in range(2) for n in range(count)
    ]
    pairs += [(fch_hbm, fch), (fcl_hbm, fcl), (frh_hbm, frh), (frl_hbm, frl)]
    pairs += [(target_hbm.at[pl.ds(own, N)], target_ref)]
    loads = [
        pltpu.make_async_copy(src, dst, load_s.at[i]) for i, (src, dst) in enumerate(pairs)
    ]
    loads[0].start()
    tall = N + 8
    my_s = lax.axis_index("space")
    s_next = lax.rem(my_s + 1, space)
    s_prev = lax.rem(my_s + space - 1, space)
    k_next = lax.rem(my_k + 1, groups)
    k_prev = lax.rem(my_k + groups - 1, groups)
    sibling = (my_s, flip(my_k, 1))
    across = (my_s, flip(my_k, 2))
    around = (flip(my_s, far), flip(my_k, 2))

    mirror = (my_s, flip(flip(my_k, 1), 2))
    has_next, has_prev = my_s < space - 1, my_s > 0
    up, down = my_k < groups - 1, my_k > 0

    barrier = pltpu.get_barrier_semaphore()
    greeted = [
        ((s_next, k_next), has_next & up), ((s_next, k_prev), has_next & down),
        ((s_prev, k_next), has_prev & up), ((s_prev, k_prev), has_prev & down),
        ((s_next, my_k), has_next), ((s_prev, my_k), has_prev),
        (around, None), (across, None), (mirror, up & down), (sibling, None),
    ]

    def when(condition, action):
        if condition is None:
            action()
        else:
            pl.when(condition)(action)

    stage = pl.when(my_s >= 0)

    expected = 0
    for device, condition in greeted:
        when(
            condition,
            functools.partial(
                pl.semaphore_signal, barrier, inc=1, device_id=device, device_id_type=MESH
            ),
        )
        expected = expected + (1 if condition is None else jnp.where(condition, 1, 0))

    for load in loads[1:]:
        load.start()

    lane = lax.broadcasted_iota(jnp.int32, (8, N), 1)[:1]

    def pack(upper, lower):
        turned = pltpu.roll(lower, H, 1)
        return jnp.where(lane < H, upper, turned), jnp.where(lane < H, turned, upper)

    def unpack(low_side, high_side):
        upper = jnp.where(lane < H, low_side, high_side)
        return upper, pltpu.roll(jnp.where(lane < H, high_side, low_side), H, 1)

    def remote(src, dst, ssem, rsem, device):
        return pltpu.make_async_remote_copy(
            src_ref=src, dst_ref=dst, send_sem=ssem, recv_sem=rsem,
            device_id=device, device_id_type=MESH,
        )

    loads[0].wait()
    after = pl.multiple_of(jnp.minimum(own + N, rows - H), H)
    before = pl.multiple_of(jnp.maximum(own - H, 0), H)
    window[0:N] = phase_ref[pl.ds(own, N)]
    window[N : N + H] = phase_ref[pl.ds(after, H)]
    window[N + H :] = phase_ref[pl.ds(before, H)]
    halo_out[0], halo_out[1] = pack(window[:N], window[N:])
    halo = [
        remote(halo_out.at[0], halo_in.at[0], halo_s.at[0], halo_r.at[0], (s_prev, my_k)),
        remote(halo_out.at[1], halo_in.at[1], halo_s.at[1], halo_r.at[1], (s_next, my_k)),
    ]

    for load in loads[1 : 1 + 2 * count]:
        load.wait()
    gains = [
        jnp.sqrt(jnp.zeros((1, N), F32) + weight_ref[n]) * 2.0**-16 for n in range(count)
    ]
    for part in range(2):
        edges = jnp.zeros((8, N), F32)
        for n in range(count):
            gain = gains[n]
            raw[0, part, tall * n : tall * n + N] = (
                pltpu.roll(kern_ref[part, n, 0:N, 0:N], H, 1) * gain
            )
            last = jnp.broadcast_to(kern_ref[part, n, N : N + 1, 0:N], (8, N))
            raw[0, part, tall * n + N : tall * (n + 1)] = pltpu.roll(last, H, 1) * gain
            for g in range(N // 8 + 1):
                end = 8 * g + 8 if g < N // 8 else N + 1
                column = kern_ref[part, n, 8 * g : end, N : N + 1]
                edges = jnp.where(lane == count * g + n, column * gain, edges)
        raw[0, part, tall * count :] = edges

    pl.semaphore_wait(barrier, expected)
    when(has_prev, halo[0].start)
    when(has_next, halo[1].start)

    theirs = flip(my_k, 2)
    to_across = remote(raw.at[0, 0], raw.at[1, 0], kern_s.at[0], kern_r.at[0], across)
    some, most = pl.ds(0, H), pl.ds(H, tall * count + 8 - H)
    to_around = remote(
        raw.at[0, 1, most], raw.at[1, 1, most], kern_s.at[1], kern_r.at[1], around
    )
    to_share = remote(
        raw.at[0, 1, some], raw.at[1, 1, some], kern_s.at[8], kern_r.at[8], across
    )
    to_around.start()
    to_across.start()
    to_share.start()

    def shared(group, number, parity, index):
        half = resp.at[group, pl.ds(0, number), pl.ds(2 * N * parity, 2 * N)]
        return remote(half, half, kern_s.at[index], kern_r.at[index], sibling)

    def passed(part, index):
        span = pl.ds(tall * (count // 2), tall * (count - count // 2) + 8)
        return remote(
            raw.at[1, part, span], raw.at[2, part, span],
            kern_s.at[index], kern_r.at[index], sibling,
        )

    first_group = [shared(my_k, count, 0, 2), shared(my_k, count, 1, 3)]
    second_half = [shared(theirs, count // 2, 0, 4), shared(theirs, count // 2, 1, 5)]
    onward = [passed(0, 6), passed(1, 7)]

    sin, cos = sincos(window[...])
    row = lax.broadcasted_iota(jnp.int32, (2 * N, N), 0)
    missing = jnp.where((row >= N) & (row < N + H) & (my_k == groups - 1), 1, 0)
    missing = jnp.where((row >= N + H) & (my_k == 0), 1, missing)
    trig[0] = jnp.where(missing == 0, cos, 0.0)
    trig[1] = jnp.where(missing == 0, sin, 0.0)

    def respond_cols(slot, chosen):
        even, odd = [], []
        edges = [raw[slot, part, tall * count :] for part in range(2)]
        for n in chosen:
            pair = [[], []]
            for part in range(2):
                turned = raw[slot, part, tall * n : tall * (n + 1)]
                extra = cat(
                    [
                        jnp.where(
                            lane == H, edges[part][:, count * g + n : count * g + n + 1], 0.0
                        )
                        for g in range(N // 8 + 1)
                    ],
                    0,
                )
                pair[0].append(turned + extra)
                pair[1].append(jnp.where(lane < H, turned, -turned) + extra)
            even.append(cat(pair[0], 1))
            odd.append(cat(pair[1], 1))
        return (
            right(cat(even, 0), fch[:, : 2 * N], fcl[:, : 2 * N]),
            right(cat(odd, 0), fch[:, 2 * N :], fcl[:, 2 * N :]),
        )

    def respond(o, slot, chosen, copies):
        ge, go = respond_cols(slot, chosen)
        row = lax.broadcasted_iota(jnp.int32, (N, 2 * N), 0)
        even, odd = [], []
        for i in range(len(chosen)):
            pair = [[], []]
            at = slice(tall * i, tall * (i + 1))
            for c in (slice(0, N), slice(N, 2 * N)):
                g = cat([ge[at, c], go[at, c]], 1)
                extra = jnp.where(row == H, g[N : N + 1], 0.0)
                pair[0].append(cat([g[H:N], g[0:H]], 0) + extra)
                pair[1].append(cat([g[H:N], -g[0:H]], 0) + extra)
            even.append(cat(pair[0], 0))
            odd.append(cat(pair[1], 0))
        for p, x in enumerate((even, odd)):
            half = slice(2 * N * p, 2 * N * (p + 1))
            r = left(frh[half], frl[half], cat(x, 1))
            for i, n in enumerate(chosen):
                resp[o, n, half] = r[:, 2 * N * i : 2 * N * (i + 1)]
            if copies:
                copies[p].start()

    def members(owners):
        return [(o, n) for o in owners for n in range(count)]

    def field_rows(owners):
        xs = []
        for o, n in members(owners):
            parts = []
            for p in range(2):
                low = slice(2 * N * p, 2 * N * p + N)
                high = slice(2 * N * p + N, 2 * N * (p + 1))
                rr, ri = resp[o, n, low], resp[o, n, high]
                sr, si = spec[low], spec[high]
                parts += [rr * sr - ri * si, rr * si + ri * sr]
            xs.append(cat(parts, 0))
        return left(fch[...], fcl[...], cat(xs, 1))

    def fields(owners):
        z = field_rows(owners)
        zs = []
        for n in range(len(owners) * count):
            q = z[:, 2 * N * n : 2 * N * (n + 1)]
            zs.append(cat([q[:N, :N], q[N:, :N], q[:N, N:], q[N:, N:]], 1))
        f = right(cat(zs, 0), frh[...], frl[...])
        for i, o in enumerate(owners):
            field[o] = f[N * count * i : N * count * (i + 1)]
        q = f * f
        total = None
        for n in range(len(owners) * count):
            g = q[N * n : N * (n + 1)]
            term = g[:, :N] + g[:, N:]
            total = term if total is None else total + term
        return total

    for load in loads[1 + 2 * count :]:
        load.wait()
    respond(my_k, 0, range(count), first_group)

    when(has_next, halo[0].wait_recv)
    when(has_prev, halo[1].wait_recv)
    upper, lower = unpack(halo_in[0], halo_in[1])
    sin, cos = sincos(cat([upper, lower], 0))
    inside = jnp.where(lane < H, space - 1 - my_s, my_s) > 0
    cos = jnp.where(inside & (missing == 0), cos, 0.0)
    sin = jnp.where(inside & (missing == 0), sin, 0.0)
    trig[2] = cos
    trig[3] = sin
    se = right(
        cat([trig[0] + cos, trig[1] + sin], 1), fch[:, : 2 * N], fcl[:, : 2 * N]
    )
    so = right(
        cat([trig[0] - cos, trig[1] - sin], 1), fch[:, 2 * N :], fcl[:, 2 * N :]
    )
    even, odd = [], []
    for c in (slice(0, N), slice(N, 2 * N)):
        g = cat([se[:, c], so[:, c]], 1)
        even.append(g[:N] + g[N:])
        odd.append(g[:N] - g[N:])
    spec[: 2 * N] = left(frh[: 2 * N], frl[: 2 * N], cat(even, 0))
    spec[2 * N :] = left(frh[2 * N :], frl[2 * N :], cat(odd, 0))

    kin, theirs_kin = flip(my_k, 1), flip(theirs, 1)
    for copy in first_group:
        copy.wait_recv()
    intensity = fields((my_k, kin))

    @stage
    def _():
        to_across.wait_recv()
        to_around.wait_recv()
        to_share.wait_recv()
        for copy in onward:
            copy.start()
        respond(theirs, 1, range(count), second_half)

    intensity = intensity + fields((theirs,))

    @stage
    def _():
        for copy in onward:
            copy.wait_recv()
        respond(theirs_kin, 2, range(count // 2, count), None)
        for copy in second_half:
            copy.wait_recv()

    intensity = intensity + fields((theirs_kin,))

    resist = 1.0 / (1.0 + jnp.exp(-STEEP * (intensity - LEVEL)))
    out_ref[0] = resist
    want = target_ref[...].astype(F32)
    factor = 4.0 * STEEP * (resist - want) * resist * (1.0 - resist)

    def pulls(owners):
        xs = []
        for o, n in members(owners):
            f = field[o, N * n : N * (n + 1)]
            xs.append(cat([factor * f[:, :N], factor * f[:, N:]], 1))
        y = right(cat(xs, 0), fch[...], fcl[...])
        xs = []
        for i in range(len(owners) * count):
            q = y[N * i : N * (i + 1)]
            re = cat([q[:, :N], q[:, 2 * N : 3 * N]], 1)
            im = cat([q[:, N : 2 * N], q[:, 3 * N :]], 1)
            xs.append(cat([re, im], 0))
        v = left(frh[...], frl[...], cat(xs, 1))
        for p in range(2):
            low = slice(2 * N * p, 2 * N * p + N)
            high = slice(2 * N * p + N, 2 * N * (p + 1))
            re, im = acc[low], acc[high]
            for i, (o, n) in enumerate(members(owners)):
                rr, ri = resp[o, n, low], resp[o, n, high]
                vr = v[low, 2 * N * i : 2 * N * (i + 1)]
                vi = v[high, 2 * N * i : 2 * N * (i + 1)]
                re = re + (rr * vr + ri * vi)
                im = im + (rr * vi - ri * vr)
            acc[low] = re
            acc[high] = im

    acc[...] = jnp.zeros((4 * N, 2 * N), F32)

    def pull_step(j, carry):
        low = jnp.where(j == 0, my_k, theirs)
        pulls((low, flip(low, 1)))
        return carry

    lax.fori_loop(0, 2, pull_step, 0)

    e = left(fch[:, : 2 * N], fcl[:, : 2 * N], acc[: 2 * N])
    o = left(fch[:, 2 * N :], fcl[:, 2 * N :], acc[2 * N :])
    u, v = e + o, e - o
    br = cat([u[:N], v[:N]], 0)
    bi = cat([u[N:], v[N:]], 0)
    e = right(cat([br[:, :N], bi[:, :N]], 1), frh[: 2 * N], frl[: 2 * N])
    o = right(cat([br[:, N:], bi[:, N:]], 1), frh[2 * N :], frl[2 * N :])
    u, v = e + o, e - o
    gout[...] = u[:, N:] * trig[0] - u[:, :N] * trig[1]
    side = v[:, N:] * trig[2] - v[:, :N] * trig[3]
    pout[0], pout[1] = pack(side[:H], side[H:N])
    quarter = H // 2
    cout[0], cout[1] = pack(side[N : N + quarter], side[N + quarter : N + H])
    cout[2], cout[3] = pack(side[N + H : N + H + quarter], side[N + H + quarter :])
    low_rows, high_rows = pl.ds(N, H), pl.ds(N + H, H)
    routes = [
        (gout.at[low_rows], (my_s, k_next), up, down),
        (gout.at[high_rows], (my_s, k_prev), down, up),
        (pout.at[0], (s_next, my_k), has_next, has_prev),
        (pout.at[1], (s_prev, my_k), has_prev, has_next),
        (cout.at[0], (s_next, k_next), has_next & up, has_prev & down),
        (cout.at[1], (s_prev, k_next), has_prev & up, has_next & down),
        (cout.at[2], (s_next, k_prev), has_next & down, has_prev & up),
        (cout.at[3], (s_prev, k_prev), has_prev & down, has_next & up),
    ]
    rims = [
        remote(src, rin.at[i] if i < 4 else cin.at[i - 4], rim_s.at[i], rim_r.at[i], device)
        for i, (src, device, _, _) in enumerate(routes)
    ]
    for i in (2, 3, 4, 5, 6, 7, 0, 1):
        when(routes[i][2], rims[i].start)
    for i in range(8):
        when(routes[i][3], rims[i].wait_recv)
    has_low = jnp.where(lane < H, my_s, space - 1 - my_s) > 0
    upper, lower = unpack(rin[2], rin[3])
    upper = upper + jnp.where(down, cat(unpack(cin[0], cin[1]), 0), 0.0)
    lower = lower + jnp.where(up, cat(unpack(cin[2], cin[3]), 0), 0.0)
    out_ref[1, :H] = (
        gout[:H] + jnp.where(my_k > 0, rin[0], 0.0) + jnp.where(has_low, upper, 0.0)
    )
    out_ref[1, H:] = (
        gout[H:N] + jnp.where(my_k < groups - 1, rin[1], 0.0) + jnp.where(has_low, lower, 0.0)
    )
    when(has_prev, halo[0].wait_send)
    when(has_next, halo[1].wait_send)
    for copy in [to_across, to_around, to_share] + first_group + second_half + onward:
        copy.wait_send()
    for i in range(8):
        when(routes[i][2], rims[i].wait_send)


def body(space, groups, phase, target, kernels, weights):
    rows, cols = phase.shape
    count = kernels.shape[1]
    far = 8 if space % 16 == 0 else 1
    consts = [jnp.asarray(t) for t in tables()]
    vmem = pl.BlockSpec(memory_space=pltpu.VMEM)
    hbm = pl.BlockSpec(memory_space=pltpu.HBM)
    dma = pltpu.SemaphoreType.DMA
    out = pl.pallas_call(
        functools.partial(kernel, space, groups, far),
        out_shape=jax.ShapeDtypeStruct((2, N, cols), F32),
        in_specs=[hbm] * 3 + [pl.BlockSpec(memory_space=pltpu.SMEM)] + [hbm] * 4,
        out_specs=vmem,
        scratch_shapes=[
            pltpu.VMEM((rows, N), F32),
            pltpu.VMEM((N, N), jnp.int32),
            pltpu.VMEM((2, count, N + 1, N + 1), F32),
        ]
        + [pltpu.VMEM(t.shape, BF16) for t in consts]
        + [
            dma((6 + 2 * count,)),
            pltpu.VMEM((2 * N, N), F32),
            pltpu.VMEM((2, N, N), F32),
            pltpu.VMEM((2, N, N), F32),
            pltpu.VMEM((4, 2 * N, N), F32),
            pltpu.VMEM((3, 2, count * (N + 8) + 8, N), F32),
            pltpu.VMEM((groups, count, 4 * N, 2 * N), F32),
            pltpu.VMEM((4 * N, 2 * N), F32),
            pltpu.VMEM((groups, count * N, 2 * N), F32),
            pltpu.VMEM((4 * N, 2 * N), F32),
            pltpu.VMEM((2 * N, N), F32),
            pltpu.VMEM((2, H, N), F32),
            pltpu.VMEM((4, H // 2, N), F32),
            pltpu.VMEM((4, H, N), F32),
            pltpu.VMEM((4, H // 2, N), F32),
            dma((2,)), dma((2,)),
            dma((9,)), dma((9,)),
            dma((8,)), dma((8,)),
        ],
        compiler_params=pltpu.CompilerParams(
            collective_id=0, has_side_effects=True, vmem_limit_bytes=int(53.8 * 2**20)
        ),
        cost_estimate=pl.CostEstimate(
            flops=14 * 10**9, bytes_accessed=4 * 10**6, transcendentals=0
        ),
        name="hopkins",
    )(phase, target, jnp.transpose(kernels, (0, 2, 1, 3)), weights, *consts)
    return (out[0], out[1])


def solution(mesh):
    placed = (P(None, "space"), P(None, "space"), P(None, "kern", None, None), P("kern"))
    return jax.shard_map(
        functools.partial(body, mesh.shape["space"], mesh.shape["kern"]),
        mesh=mesh,
        in_specs=placed,
        out_specs=(P("kern", "space"), P("kern", "space")),
        check_vma=False,
    )
```
